128 devices in a mesh: px: 16 (over z_hi, x, core), py: 8 (over z_lo, y).
Axes of the slice: x: 4, y: 4, z: 4 (z_hi: 2, z_lo: 2; z = z_hi * 2 + z_lo), core: 2. Of those that a mesh axis runs over, the one named last changes fastest.
Arguments:
- cotangent: float32 [128, 128, 128], P('px', 'py'), may hold values from -6 to 6
- fraction: float32 [3, 128, 128, 128], P(None, 'px', 'py'), may hold values from 0 to 0.999
- grid_base: int32 [3, 128, 128, 128], P(None, 'px', 'py'), may hold values from 0 to 511, as said below
- cell_count: int32 [128, 128], P('px', 'py'), may hold values from 32 to 128, as said below
- influence: float32 [256, 512, 512], P(('px', 'py')), as said below
Outputs:
- charge_gradient: float32 [128, 128, 128], P('px', 'py')
The draws below stay inside these ranges and needn't reach their ends.
Inputs may be any that keep to these rules, and one draw needn't show every extreme that they name: grid_base[0] // 4 is the cell's first index and grid_base[1] // 4 its second; grid_base[2] lies in 0 to 255. `cell_count`: some cell is full. Positive and even: influence[kz, kx, ky] equals influence[-kz, -kx, -ky], wave numbers taken modulo 256, 512, 512.
All inputs are finite; a program needn't handle non-finite values.
Results may differ from the reference program's by a relative error of at most 0.0003.
Values sent between devices are 32-bit elements; how exact they have to be, the bound alone decides.
No kernel may reach another device: no remote copies, remote signals or barrier semaphores. Data moves between devices by JAX's collectives and lax.ppermute only.
A program may use at most 128 MiB of HBM per device.

```python
import math
import jax
import jax.numpy as jnp
from jax import lax

NZ = 256
CELL = 4
SLOTS = 128
NX = 512
NY = 512
NCX = 128
NCY = 128


def draw_grid_base(key, part):
    key = jax.random.fold_in(key, 11)
    first_key, second_key, third_key = jax.random.split(key, 3)
    atom_shape = (NCX, NCY, SLOTS)
    start_x = (jnp.arange(NCX, dtype=jnp.int32) * CELL)[:, None, None]
    start_y = (jnp.arange(NCY, dtype=jnp.int32) * CELL)[None, :, None]
    along_x = start_x + jax.random.randint(first_key, atom_shape, 0, CELL, dtype=jnp.int32)
    along_y = start_y + jax.random.randint(second_key, atom_shape, 0, CELL, dtype=jnp.int32)
    along_z = jax.random.randint(third_key, atom_shape, 0, NZ, dtype=jnp.int32)
    along_x = along_x.at[NCX - 1, 0, 0].set(NX - 1).at[0, 0, 1].set(0)
    along_y = along_y.at[0, NCY - 1, 0].set(NY - 1).at[0, 0, 1].set(0)
    along_z = along_z.at[0, 0, 0].set(NZ - 1).at[0, 0, 1].set(0)
    return jnp.stack([along_x, along_y, along_z]).astype(jnp.int32)


def draw_cell_count(key, part):
    key = jax.random.fold_in(key, 23)
    first_key, second_key = jax.random.split(key, 2)
    cells_total = NCX * NCY
    counts = jax.random.randint(first_key, (cells_total,), max(1, SLOTS // 4), SLOTS + 1, dtype=jnp.int32)
    chosen = jax.random.randint(second_key, (), 0, cells_total, dtype=jnp.int32)
    counts = jnp.where(jnp.arange(cells_total, dtype=jnp.int32) == chosen, SLOTS, counts)
    return counts.reshape(NCX, NCY).astype(jnp.int32)


def wave_numbers(length):
    indices = jnp.arange(length, dtype=jnp.int32)
    return jnp.minimum(indices, length - indices).astype(jnp.float32) / length


def draw_influence(key, part):
    key = jax.random.fold_in(key, 37)
    along_z = wave_numbers(NZ)[:, None, None]
    along_x = wave_numbers(NX)[None, :, None]
    along_y = wave_numbers(NY)[None, None, :]
    squared = along_z * along_z + along_x * along_x + along_y * along_y
    envelope = 0.3 / (squared + 1.0 / (NX * NY)) + 10.0
    raw = jax.random.uniform(key, (NZ, NX, NY), jnp.float32, 0.0, 1.0)
    mirror = jnp.roll(jnp.flip(raw, (0, 1, 2)), 1, axis=(0, 1, 2))
    even = 0.5 * (raw + mirror)
    factor = jnp.exp(math.log(0.5) + math.log(4.0) * even)
    return (factor * envelope).astype(jnp.float32)


def steps_of(key, shape, shards, smallest, high):
    level, own = 1.0, jax.random.fold_in(key, 6)
    for dim, blocks in shards:
        steps = jnp.exp(jax.random.uniform(jax.random.fold_in(own, dim), (blocks,), jnp.float32, smallest / len(shards), high / len(shards)))
        level = level * jnp.repeat(steps, shape[dim] // blocks).reshape([-1 if axis == dim else 1 for axis in range(len(shape))])
    return level


def scatter_about(stream_key, shape, width, limit, cuts=(), held_as=jnp.bfloat16):
    values = jax.random.normal(stream_key, shape, jnp.float32) * width
    if len(cuts) > 0:
        values = steps_of(stream_key, shape, cuts, -0.22, 0.18) * values
    return jnp.clip(values, min=-limit, max=limit).astype(held_as)


def setup_inputs(seed: int = 0) -> dict:
    streams_of = jax.random.split(jax.random.key(seed), 6)
    return {
        "cotangent": scatter_about(streams_of[0], (NCX, NCY, SLOTS), 1.0, 6.0, ((0, 16), (1, 8)), jnp.float32),
        "fraction": jnp.clip(0.999 * jax.random.uniform(streams_of[1], (3, NCX, NCY, SLOTS), jnp.float32) ** steps_of(streams_of[1], (3, NCX, NCY, SLOTS), ((1, 16), (2, 8)), -0.2, 0.2), 0.0, 0.999),
        "grid_base": draw_grid_base(jax.random.fold_in(streams_of[5], 71), 0),
        "cell_count": draw_cell_count(jax.random.fold_in(streams_of[5], 71), 0),
        "influence": draw_influence(jax.random.fold_in(streams_of[5], 71), 0),
    }


def spline_weights(fractions):
    nothing = jnp.zeros_like(fractions)
    values = [fractions, 1.0 - fractions]
    for degree in (3, 4, 5):
        updated = []
        for position in range(degree):
            upper_term = values[position] if position < degree - 1 else nothing
            lower_term = values[position - 1] if position >= 1 else nothing
            updated.append(((fractions + position) * upper_term + (degree - fractions - position) * lower_term) / (degree - 1))
        values = updated
    return jnp.stack(values)


def reference(cotangent, fraction, grid_base, cell_count, influence):
    slot_ids = jnp.arange(SLOTS, dtype=jnp.int32)
    occupied = slot_ids[None, None, :] < cell_count[:, :, None]
    charge = jnp.where(occupied, cotangent, jnp.zeros_like(cotangent))
    shifts = 2 - jnp.arange(5, dtype=jnp.int32)
    frac_rows = jnp.moveaxis(fraction, 1, 0)
    base_rows = jnp.moveaxis(grid_base, 1, 0)

    def points(frac_row, base_row):
        index_x = ((base_row[0][None] + shifts[:, None, None]) % NX).astype(jnp.int32)
        index_y = ((base_row[1][None] + shifts[:, None, None]) % NY).astype(jnp.int32)
        index_z = ((base_row[2][None] + shifts[:, None, None]) % NZ).astype(jnp.int32)
        across_x = spline_weights(frac_row[0])[:, None, None]
        across_y = spline_weights(frac_row[1])[None, :, None]
        across_z = spline_weights(frac_row[2])[None, None, :]
        indices = (index_x[:, None, None], index_y[None, :, None], index_z[None, None, :])
        return indices, across_x, across_y, across_z

    def spread_step(mesh_grid, row):
        charge_row, frac_row, base_row = row
        indices, across_x, across_y, across_z = points(frac_row, base_row)
        values = ((charge_row * across_x) * across_y) * across_z
        return mesh_grid.at[indices].add(values), None

    spread, unused = lax.scan(spread_step, jnp.zeros((NX, NY, NZ), jnp.float32), (charge, frac_rows, base_rows))
    spectrum = jnp.fft.fftn(spread)
    scaled = spectrum * jnp.transpose(influence, (1, 2, 0))
    potential = jnp.real(jnp.fft.ifftn(scaled)).astype(jnp.float32)

    def gather_step(carry, row):
        frac_row, base_row = row
        indices, across_x, across_y, across_z = points(frac_row, base_row)
        values = potential[indices] * ((across_x * across_y) * across_z)
        return carry, jnp.sum(values, axis=(0, 1, 2))

    unused_carry, gradient = lax.scan(gather_step, jnp.zeros((), jnp.float32), (frac_rows, base_rows))
    return jnp.where(occupied, gradient, jnp.zeros_like(gradient))
```

```python
import jax
import jax.numpy as jnp
import ml_dtypes
import numpy as np
from jax import lax
from jax.experimental import pallas as pl
from jax.experimental.pallas import tpu as pltpu
from jax.sharding import PartitionSpec as P

NX, NY, NZ = 512, 512, 256
PX, PY = 16, 8
DEVICES = PX * PY
MIDDLE = DEVICES // 2
CELLS = 128
ROWS = 40
EXT_X, EXT_Y = 40, 72
BF, F32 = jnp.bfloat16, jnp.float32


def split_np(table):
    high = table.astype(ml_dtypes.bfloat16)
    low = (table - high.astype(np.float64)).astype(ml_dtypes.bfloat16)
    return high, low


def depth_angles():
    device = np.arange(DEVICES)
    wave = np.where(device < MIDDLE, 2 * device + 1, 2 * device)
    return 2.0 * np.pi * ((wave[:, None] * np.arange(NZ)[None, :]) % NZ) / NZ


def depth_tables():
    angle = depth_angles()
    first, second = np.cos(angle), -np.sin(angle)
    second[MIDDLE] = 1.0
    forward = np.concatenate([first, second])
    gain = np.full((DEVICES, 1), 2.0)
    gain[MIDDLE] = 1.0
    inverse = forward * np.concatenate([gain, gain]) / (NX * NY * NZ)
    return np.concatenate(split_np(forward)), np.concatenate(split_np(inverse))


def y_tables():
    tables = []
    for parity in (0, 1):
        wave = 2 * np.arange(256) + parity
        main = 64 * np.arange(4)[:, None] + np.arange(64)[None, :]
        rim = (64 * (np.arange(8)[:, None] + 1) + np.arange(4)[None, :]) % NY

        def pair(position):
            angle = 2.0 * np.pi * ((position[..., None] * wave) % NY) / NY
            cosine, sine = np.cos(angle), np.sin(angle)
            first = np.concatenate([cosine, -sine], axis=-1)
            second = np.concatenate([sine, cosine], axis=-1)
            return first, second

        first, second = pair(main)
        whole = np.stack([first, second], axis=1).reshape(512, 512)
        first, second = pair(rim)
        edge = np.stack([first, second], axis=0).reshape(64, 512)
        whole = np.concatenate([whole, edge, np.zeros((64, 512))])
        tables.append(np.stack(split_np(whole)))
    return np.stack(tables)


def x_tables():
    forward, inverse = [], []
    for parity in (0, 1):
        wave = 2 * np.arange(256) + parity
        angle = 2.0 * np.pi * ((wave[:, None] * np.arange(256)[None, :]) % NX) / NX
        cosine, sine = np.cos(angle), np.sin(angle)
        forward.append(np.concatenate(split_np(np.concatenate([cosine, sine]))))
        inverse.append(np.concatenate(split_np(np.concatenate([cosine.T, sine.T]))))
    return np.stack(forward + inverse)


def turn_tables():
    index = np.arange(256)
    even = np.zeros((256, 256))
    even[index, (256 - index) % 256] = 1.0
    odd = np.zeros((256, 256))
    odd[index, 255 - index] = 1.0
    return np.stack([even, odd]).astype(ml_dtypes.bfloat16)


def sort_table():
    index = np.arange(512)
    order = np.zeros((512, 512))
    order[index, (index % 2) * 256 + index // 2] = 1.0
    return order.astype(ml_dtypes.bfloat16)


def split(value):
    high = value.astype(BF)
    low = (value - high.astype(F32)).astype(BF)
    return high, low


def dot(left, right):
    return lax.dot_general(left, right, (((1,), (0,)), ((), ())), preferred_element_type=F32)


def dot_nt(left, right):
    return lax.dot_general(left, right, (((1,), (1,)), ((), ())), preferred_element_type=F32)


def spline_weights(fractions):
    values = [fractions, 1.0 - fractions]
    for degree in (3, 4, 5):
        updated = []
        for position in range(degree):
            term = None
            if position < degree - 1:
                term = (fractions + float(position)) * values[position]
            if position >= 1:
                lower = (float(degree - position) - fractions) * values[position - 1]
                term = lower if term is None else term + lower
            updated.append(term * (1.0 / (degree - 1)))
        values = updated
    return values


def pick(selected, weights):
    total = jnp.where(selected == 4, weights[4], 0.0)
    for degree in (3, 2, 1, 0):
        total = jnp.where(selected == degree, weights[degree], total)
    return total


def occupied_rows(count_ref, chunk):
    sub = lax.broadcasted_iota(jnp.int32, (8, 128), 0)
    slot = lax.broadcasted_iota(jnp.int32, (8, 128), 1)
    counts = jnp.zeros((8, 128), jnp.int32)
    for row in range(8):
        counts = jnp.where(sub == row, count_ref[chunk // 2, (chunk % 2) * 8 + row], counts)
    return slot < counts


def prepare(frac_ref, base_ref, wx_ref, wy_ref, wz_ref, charge_of):
    def chunk_step(chunk, carry):
        rows = pl.ds(pl.multiple_of(chunk * 8, 8), 8)
        weights = spline_weights(frac_ref[0, rows, :])
        offset = (base_ref[0, rows, :] & 3) + 4
        charge = charge_of(chunk, rows)
        for position in range(8):
            window = pick(offset - position, weights)
            wx_ref[position, rows, :] = window if charge is None else window * charge
        for degree, weight in enumerate(spline_weights(frac_ref[1, rows, :])):
            wy_ref[degree, rows, :] = weight
        for degree, weight in enumerate(spline_weights(frac_ref[2, rows, :])):
            wz_ref[degree, rows, :] = weight
        return carry

    lax.fori_loop(0, CELLS // 8, chunk_step, 0)


def depth_weights(base_ref, wz_ref, cell):
    row = pl.ds(cell, 1)
    level = lax.broadcasted_iota(jnp.int32, (NZ, 128), 0)
    selected = ((base_ref[2, row, :] + 2) - level) & (NZ - 1)
    return split(pick(selected, [wz_ref[degree, row, :] for degree in range(5)]))


def pair_depth(base_ref, wz_ref, cell):
    first = depth_weights(base_ref, wz_ref, cell)
    second = depth_weights(base_ref, wz_ref, cell + 1)
    return (
        jnp.concatenate([first[0], second[0]], axis=1),
        jnp.concatenate([first[1], second[1]], axis=1),
    )


def pair_window_y(base_ref, wy_ref, cell):
    parts = []
    for side in (0, 1):
        row = pl.ds(cell + side, 1)
        position = lax.broadcasted_iota(jnp.int32, (16, 128), 0)
        selected = ((base_ref[1, row, :] & 3) + 4 + 4 * side) - position
        parts.append(pick(selected, [wy_ref[degree, row, :] for degree in range(5)]))
    return jnp.concatenate(parts, axis=1)


def pair_row(ref, position, cell):
    return jnp.concatenate(
        [ref[position, pl.ds(cell, 1), :], ref[position, pl.ds(cell + 1, 1), :]], axis=1
    )


def spread_kernel(
    count_ref, cot_ref, frac_ref, base_ref, table_ref, out_ref, ext_ref, wx_ref, wy_ref, wz_ref
):
    def charge_of(chunk, rows):
        return jnp.where(occupied_rows(count_ref, chunk), cot_ref[rows, :], 0.0)

    prepare(frac_ref, base_ref, wx_ref, wy_ref, wz_ref, charge_of)

    def clear(step, carry):
        rows = pl.ds(pl.multiple_of(step * EXT_Y, 8), EXT_Y)
        for half in (0, 1):
            ext_ref[half, rows, :] = jnp.zeros((EXT_Y, 128), F32)
        return carry

    lax.fori_loop(0, EXT_X, clear, 0)

    def pair_step(step, carry):
        cell_x, pair = step // 8, step % 8
        cell = step * 2
        depth_high, depth_low = pair_depth(base_ref, wz_ref, cell)
        window_y = pair_window_y(base_ref, wy_ref, cell)
        lifted = jnp.concatenate(
            [pair_row(wx_ref, u, cell) * window_y for u in range(8)], axis=0
        )
        high, low = split(lifted)
        both = dot_nt(jnp.concatenate([high, low], axis=0), depth_high)
        patch = both[:128] + both[128:] + dot_nt(high, depth_low)
        for u in range(8):
            rows = pl.ds(pl.multiple_of((cell_x * 4 + u) * EXT_Y + pair * 8, 8), 16)
            for half in (0, 1):
                ext_ref[half, rows, :] += patch[16 * u : 16 * u + 16, 128 * half : 128 * half + 128]
        return carry

    lax.fori_loop(0, CELLS // 2, pair_step, 0)

    lane = lax.broadcasted_iota(jnp.int32, (128, 128), 1)

    def transform(blocks, first_row):
        high, low = split(jnp.concatenate(blocks, axis=0))
        both = dot_nt(table_ref[...], high)
        planes = both[:256] + both[256:] + dot_nt(table_ref[:256], low)
        for duo in (0, 1):
            first = planes[:128, 128 * duo : 128 * duo + 128]
            second = planes[128:, 128 * duo : 128 * duo + 128]
            left = jnp.where(lane < 64, first, pltpu.roll(second, 64, 1))
            right = jnp.where(lane < 64, pltpu.roll(first, 64, 1), second)
            out_ref[pl.ds(first_row + 2 * duo, 128, stride=ROWS), :] = left
            out_ref[pl.ds(first_row + 2 * duo + 1, 128, stride=ROWS), :] = right

    def row_step(step, carry):
        blocks = []
        for row in range(4):
            rows = pl.ds(pl.multiple_of((step * 4 + row) * EXT_Y, 8), 64)
            blocks.append(jnp.concatenate([ext_ref[0, rows, :], ext_ref[1, rows, :]], axis=1))
        transform(blocks, step * 4)
        return carry

    lax.fori_loop(0, 9, row_step, 0)
    blocks = []
    for rim in range(4):
        rows = pl.ds(64 + rim, EXT_X, stride=EXT_Y)
        block = jnp.concatenate([ext_ref.at[0][rows, :], ext_ref.at[1][rows, :]], axis=1)
        blocks.append(jnp.concatenate([block, jnp.zeros((24, 256), F32)], axis=0))
    transform(blocks, 36)


def plane_kernel(
    flag_ref,
    in_ref,
    influence_hbm,
    zero_hbm,
    y_hbm,
    x_hbm,
    turn_hbm,
    sort_hbm,
    out_ref,
    influence,
    zero_plane,
    y_table,
    x_table,
    turn,
    sort,
    block_high,
    block_low,
    sorted_influence,
    sorted_difference,
    spectrum,
    result,
    sems,
):
    plane, middle = flag_ref[0], flag_ref[1]
    moves = [(sort_hbm, sort), (y_hbm, y_table), (x_hbm, x_table), (turn_hbm, turn)]
    for part in range(4):
        columns = pl.ds(128 * part, 128)
        moves.append((influence_hbm.at[plane, :, columns], influence.at[part]))
        moves.append((zero_hbm.at[:, columns], zero_plane.at[part]))
    copies = [
        pltpu.make_async_copy(source, target, sems.at[index])
        for index, (source, target) in enumerate(moves)
    ]
    for copy in copies:
        copy.start()

    sub = lax.broadcasted_iota(jnp.int32, (8, 128), 0)
    lane = lax.broadcasted_iota(jnp.int32, (32, 128), 1)
    lane8 = lax.broadcasted_iota(jnp.int32, (8, 128), 1)

    def block_rows(p, q, first, count):
        return pl.ds(pl.multiple_of((p * PY + q) * ROWS + first, 8), count)

    def rim_rows(p):
        tiles = []
        for q in range(0, PY, 2):
            even = in_ref[block_rows(p, q, 32, 8), :]
            odd = in_ref[block_rows(p, q + 1, 32, 8), :]
            tiles.append(jnp.where(sub < 4, pltpu.roll(even, 4, 0), odd))
        tiles.append(jnp.zeros((96, 128), F32))
        return jnp.concatenate(tiles, axis=0).T

    def main_rows(p, q):
        own = in_ref[block_rows(p, q, 0, 32), :]
        edge = in_ref[block_rows((p + PX - 1) % PX, q, 32, 8), :]
        return jnp.concatenate([own[:8] + jnp.where(sub < 4, edge, 0.0), own[8:]], axis=0)

    def edge_rows(p):
        turned, before = rim_rows(p), rim_rows((p + PX - 1) % PX)
        own = turned[0:32] + pltpu.roll(turned[64:96], 32, 1)
        edge = before[32:40] + pltpu.roll(before[96:104], 32, 1)
        first = own[:8] + jnp.where(sub < 4, edge, 0.0)
        return jnp.concatenate([first, own[8:]], axis=0)

    def assemble(p, carry):
        rows = pl.ds(pl.multiple_of(p * 32, 32), 32)

        def put(parity, columns, value):
            high, low = split(value)
            block_high[parity, rows, columns] = high
            block_low[parity, rows, columns] = low

        for q in range(4):
            columns = pl.ds(128 * q, 128)
            a, b = main_rows(p, q), main_rows(p, q + 4)
            c, d = main_rows(p + 8, q), main_rows(p + 8, q + 4)
            even, odd = a + b, a - b
            even_far, odd_far = c + d, c - d
            put(0, columns, even + even_far)
            put(1, columns, odd + odd_far)
            put(2, columns, even - even_far)
            put(3, columns, odd - odd_far)
        near, far = edge_rows(p), edge_rows(p + 8)
        columns = pl.ds(512, 128)
        for parity in (0, 1):
            put(parity, columns, near + far)
            put(parity + 2, columns, near - far)
        return carry

    lax.fori_loop(0, 8, assemble, 0)

    def sorted_columns(value):
        high, low = split(value)
        return dot(high, sort[...]) + dot(low, sort[...])

    for copy in copies:
        copy.wait()

    half = middle.astype(F32) * 0.5
    for f in (0, 1):
        rows = pl.ds(f, 256, stride=2)
        own = jnp.concatenate([influence.at[part][rows, :] for part in range(4)], axis=1)
        for_sorting = own

        @pl.when(middle == 0)
        def _plain():
            value = sorted_columns(for_sorting)
            for e in (0, 1):
                sorted_influence[2 * f + e] = value[:, 256 * e : 256 * e + 256]

        @pl.when(middle != 0)
        def _mixed():
            other = jnp.concatenate([zero_plane.at[part][rows, :] for part in range(4)], axis=1)
            total = sorted_columns((for_sorting + other) * half)
            difference = sorted_columns((for_sorting - other) * half)
            for e in (0, 1):
                sorted_influence[2 * f + e] = total[:, 256 * e : 256 * e + 256]
                sorted_difference[2 * f + e] = difference[:, 256 * e : 256 * e + 256]

    def left_products(table, value):
        high, low = split(value)
        both = dot(table, high)
        total = both[:512] + both[512:] + dot(table[:512], low)
        return total[:256], total[256:]

    for f in (0, 1):
        for e in (0, 1):
            which = 2 * f + e
            high, low = block_high[which], block_low[which]
            table_high, table_low = y_table[e, 0], y_table[e, 1]
            both = dot(jnp.concatenate([high, low], axis=0), table_high)
            along_y = both[:256] + both[256:] + dot(high, table_low)
            forward = x_table[f]
            cos_re, sin_re = left_products(forward, along_y[:, :256])
            cos_im, sin_im = left_products(forward, along_y[:, 256:])
            real, imag = cos_re + sin_im, cos_im - sin_re
            weight = sorted_influence[which]
            spectrum[0] = real * weight
            spectrum[1] = imag * weight

            @pl.when(middle != 0)
            def _add_turned():
                def turned(value):
                    high, low = split(value)
                    part = dot(turn[f], high) + dot(turn[f], low)
                    high, low = split(part)
                    return dot(high, turn[e]) + dot(low, turn[e])

                weight = sorted_difference[which]
                spectrum[0] += turned(real) * weight
                spectrum[1] -= turned(imag) * weight

            inverse = x_table[2 + f]
            cos_re, sin_re = left_products(inverse, spectrum[0])
            cos_im, sin_im = left_products(inverse, spectrum[1])
            back = jnp.concatenate([cos_re - sin_im, cos_im + sin_re], axis=1)
            high, low = split(back)
            both = dot_nt(jnp.concatenate([high, low], axis=0), table_high)
            result[which] = both[:256] + both[256:] + dot_nt(high, table_low)

    def four(rows, columns):
        a, b = result[0, rows, columns], result[1, rows, columns]
        c, d = result[2, rows, columns], result[3, rows, columns]
        return a, b, c, d

    def send(p, carry):
        rows = pl.ds(pl.multiple_of(p * 32, 32), 32)
        after = pl.ds(pl.multiple_of(((p + 1) % 8) * 32, 32), 8)
        wrap = jnp.where(p == 7, -1.0, 1.0)
        columns = pl.ds(512, 128)
        a, b, c, d = four(rows, columns)
        a1, b1, c1, d1 = four(after, columns)
        rims = []
        for sign in (1.0, -1.0):
            own = (a + b) + sign * (c + d)
            edge = (a1 + b1) + (sign * wrap) * (c1 + d1)
            tall = jnp.concatenate([own, edge, jnp.zeros((88, 128), F32)], axis=0).T
            rims.append(tall[0:32] + pltpu.roll(tall[32:64], 64, 1))
        for q in range(4):
            columns = pl.ds(128 * q, 128)
            a, b, c, d = four(rows, columns)
            a1, b1, c1, d1 = four(after, columns)
            for side, y_sign in ((0, 1.0), (4, -1.0)):
                even, odd = a + y_sign * b, c + y_sign * d
                even1, odd1 = a1 + y_sign * b1, c1 + y_sign * d1
                for far, x_sign in ((0, 1.0), (8, -1.0)):
                    target_q, target_p = q + side, p + far
                    out_ref[block_rows(target_p, target_q, 0, 32), :] = even + x_sign * odd
                    edge = even1 + (x_sign * wrap) * odd1
                    tile = rims[far // 8][8 * (target_q // 2) : 8 * (target_q // 2) + 8]
                    if target_q % 2 == 0:
                        tile = pltpu.roll(tile, 4, 0)
                    out_ref[block_rows(target_p, target_q, 32, 8), :] = jnp.where(
                        sub < 4, edge, tile
                    )
        return carry

    lax.fori_loop(0, 8, send, 0)


def gather_kernel(
    count_ref, in_ref, frac_ref, base_ref, table_ref, out_ref, ext_ref, wx_ref, wy_ref, wz_ref
):
    prepare(frac_ref, base_ref, wx_ref, wy_ref, wz_ref, lambda chunk, rows: None)

    def inverse(first_row):
        blocks = []
        for row in range(4):
            block = in_ref[pl.ds(first_row + row, 128, stride=ROWS), :].T
            blocks.append(jnp.concatenate([block[:64], block[64:]], axis=1))
        high, low = split(jnp.concatenate(blocks, axis=0))
        both = dot(jnp.concatenate([high, low], axis=0), table_ref[:256])
        return both[:256] + both[256:] + dot(high, table_ref[256:])

    def row_step(step, carry):
        values = inverse(step * 4)
        for row in range(4):
            start = (step * 4 + row) * EXT_Y
            rows = pl.ds(pl.multiple_of(start, 8), 64)
            last = pl.ds(pl.multiple_of(start + 64, 8), 8)
            for half in (0, 1):
                ext_ref[half, rows, :] = values[64 * row : 64 * row + 64, 128 * half : 128 * half + 128]
                ext_ref[half, last, :] = jnp.zeros((8, 128), F32)
        return carry

    lax.fori_loop(0, 9, row_step, 0)
    values = inverse(36)
    for rim in range(4):
        rows = pl.ds(64 + rim, EXT_X, stride=EXT_Y)
        for half in (0, 1):
            ext_ref.at[half][rows, :] = values[64 * rim : 64 * rim + EXT_X, 128 * half : 128 * half + 128]

    def pair_step(step, carry):
        cell_x, pair = step // 8, step % 8
        cell = step * 2
        depth_high, depth_low = pair_depth(base_ref, wz_ref, cell)
        windows = []
        for u in range(8):
            rows = pl.ds(pl.multiple_of((cell_x * 4 + u) * EXT_Y + pair * 8, 8), 16)
            windows.append(jnp.concatenate([ext_ref[0, rows, :], ext_ref[1, rows, :]], axis=1))
        high, low = split(jnp.concatenate(windows, axis=0))
        both = dot(jnp.concatenate([high, low], axis=0), depth_high)
        part = both[:128] + both[128:] + dot(high, depth_low)
        total = part[:16] * pair_row(wx_ref, 0, cell)
        for u in range(1, 8):
            total += part[16 * u : 16 * u + 16] * pair_row(wx_ref, u, cell)
        total = jnp.sum(total * pair_window_y(base_ref, wy_ref, cell), axis=0, keepdims=True)
        out_ref[pl.ds(cell, 1), :] = total[:, :128]
        out_ref[pl.ds(cell + 1, 1), :] = total[:, 128:]
        return carry

    lax.fori_loop(0, CELLS // 2, pair_step, 0)

    def mask_step(chunk, carry):
        rows = pl.ds(pl.multiple_of(chunk * 8, 8), 8)
        out_ref[rows, :] = jnp.where(occupied_rows(count_ref, chunk), out_ref[rows, :], 0.0)
        return carry

    lax.fori_loop(0, CELLS // 8, mask_step, 0)


VMEM = pl.BlockSpec(memory_space=pltpu.VMEM)
SMEM = pl.BlockSpec(memory_space=pltpu.SMEM)
ANY = pl.BlockSpec(memory_space=pl.ANY)
PARAMS = pltpu.CompilerParams(vmem_limit_bytes=56 * 1024 * 1024)


def cell_scratch():
    return [
        pltpu.VMEM((2, EXT_X * EXT_Y, 128), F32),
        pltpu.VMEM((8, CELLS, 128), F32),
        pltpu.VMEM((5, CELLS, 128), F32),
        pltpu.VMEM((5, CELLS, 128), F32),
    ]


def per_device(cotangent, fraction, grid_base, cell_count, influence):
    device = lax.axis_index("px") * PY + lax.axis_index("py")
    flags = jnp.stack([(device < MIDDLE).astype(jnp.int32), (device == MIDDLE).astype(jnp.int32)])
    zero_plane = lax.ppermute(influence[0], ("px", "py"), [(0, MIDDLE)])
    fraction = fraction.reshape(3, CELLS, 128)
    grid_base = grid_base.reshape(3, CELLS, 128)
    forward_z, inverse_z = depth_tables()

    sent = pl.pallas_call(
        spread_kernel,
        out_shape=jax.ShapeDtypeStruct((DEVICES * ROWS, 128), F32),
        in_specs=[SMEM, VMEM, VMEM, VMEM, VMEM],
        out_specs=VMEM,
        scratch_shapes=cell_scratch(),
        compiler_params=PARAMS,
        cost_estimate=pl.CostEstimate(flops=10**10, bytes_accessed=10**7, transcendentals=0),
        name="spread",
    )(cell_count, cotangent.reshape(CELLS, 128), fraction, grid_base, forward_z)

    def exchange(array):
        array = array.reshape(DEVICES, ROWS, 128)
        array = lax.all_to_all(array, ("px", "py"), split_axis=0, concat_axis=0, tiled=True)
        return array.reshape(DEVICES * ROWS, 128)

    sent, zero_plane = lax.optimization_barrier((sent, zero_plane))
    planes = exchange(sent)
    back = pl.pallas_call(
        plane_kernel,
        out_shape=jax.ShapeDtypeStruct((DEVICES * ROWS, 128), F32),
        in_specs=[SMEM, VMEM, ANY, ANY, ANY, ANY, ANY, ANY],
        out_specs=VMEM,
        scratch_shapes=[
            pltpu.VMEM((4, 512, 128), F32),
            pltpu.VMEM((4, 512, 128), F32),
            pltpu.VMEM((2, 2, 640, 512), BF),
            pltpu.VMEM((4, 1024, 256), BF),
            pltpu.VMEM((2, 256, 256), BF),
            pltpu.VMEM((512, 512), BF),
            pltpu.VMEM((4, 256, 640), BF),
            pltpu.VMEM((4, 256, 640), BF),
            pltpu.VMEM((4, 256, 256), F32),
            pltpu.VMEM((4, 256, 256), F32),
            pltpu.VMEM((2, 256, 256), F32),
            pltpu.VMEM((4, 256, 640), F32),
            pltpu.SemaphoreType.DMA((12,)),
        ],
        compiler_params=PARAMS,
        name="planes",
    )(
        flags,
        planes,
        influence,
        zero_plane,
        y_tables(),
        x_tables(),
        turn_tables(),
        sort_table(),
    )
    returned = exchange(back)

    gradient = pl.pallas_call(
        gather_kernel,
        out_shape=jax.ShapeDtypeStruct((CELLS, 128), F32),
        in_specs=[SMEM, VMEM, VMEM, VMEM, VMEM],
        out_specs=VMEM,
        scratch_shapes=cell_scratch(),
        compiler_params=PARAMS,
        name="gather",
    )(cell_count, returned, fraction, grid_base, inverse_z)
    return gradient.reshape(cotangent.shape)


def solution(mesh):
    placed = (
        P("px", "py", None),
        P(None, "px", "py", None),
        P(None, "px", "py", None),
        P("px", "py"),
        P(("px", "py"), None, None),
    )
    return jax.shard_map(
        per_device, mesh=mesh, in_specs=placed, out_specs=P("px", "py", None), check_vma=False
    )
```

```python
import jax
import jax.numpy as jnp
import ml_dtypes
import numpy as np
from jax import lax
from jax.experimental import pallas as pl
from jax.experimental.pallas import tpu as pltpu
from jax.sharding import PartitionSpec as P

NX, NY, NZ = 512, 512, 256
PX, PY = 16, 8
DEVICES = PX * PY
MIDDLE = DEVICES // 2
CELLS = 128
ROWS = 40
EXT_X, EXT_Y = 40, 72
BF, F32 = jnp.bfloat16, jnp.float32


def split_np(table):
    high = table.astype(ml_dtypes.bfloat16)
    low = (table - high.astype(np.float64)).astype(ml_dtypes.bfloat16)
    return high, low


def depth_angles():
    device = np.arange(DEVICES)
    wave = np.where(device < MIDDLE, 2 * device + 1, 2 * device)
    return 2.0 * np.pi * ((wave[:, None] * np.arange(NZ)[None, :]) % NZ) / NZ


def depth_tables():
    angle = depth_angles()
    first, second = np.cos(angle), -np.sin(angle)
    second[MIDDLE] = 1.0
    forward = np.concatenate([first, second])
    gain = np.full((DEVICES, 1), 2.0)
    gain[MIDDLE] = 1.0
    inverse = forward * np.concatenate([gain, gain]) / (NX * NY * NZ)
    return np.concatenate(split_np(forward)), np.concatenate(split_np(inverse))


def y_tables():
    tables = []
    for residue in range(4):
        wave = 4 * np.arange(128) + residue
        main = 64 * np.arange(2)[:, None] + np.arange(64)[None, :]
        rim = (64 * (np.arange(8)[:, None] + 1) + np.arange(4)[None, :]) % NY

        def pair(position):
            angle = 2.0 * np.pi * ((position[..., None] * wave) % NY) / NY
            cosine, sine = np.cos(angle), np.sin(angle)
            first = np.concatenate([cosine, -sine], axis=-1)
            second = np.concatenate([sine, cosine], axis=-1)
            return first, second

        whole = np.stack(pair(main), axis=1).reshape(256, 256)
        edge = np.stack(pair(rim), axis=0).reshape(64, 256)
        whole = np.concatenate([whole, edge, np.zeros((64, 256))])
        tables.extend(split_np(whole))
    return np.concatenate(tables)


def x_tables():
    forward, inverse = [], []
    for parity in (0, 1):
        wave = 2 * np.arange(256) + parity
        angle = 2.0 * np.pi * ((wave[:, None] * np.arange(256)[None, :]) % NX) / NX
        cosine, sine = np.cos(angle), np.sin(angle)
        forward.append(np.concatenate(split_np(np.concatenate([cosine, sine]))))
        inverse.append(np.concatenate(split_np(np.concatenate([cosine.T, sine.T]))))
    return np.concatenate(forward + inverse[1:])


def turn_tables():
    tables = []
    for size in (256, 128):
        index = np.arange(size)
        for shift in (0, 1):
            table = np.zeros((size, size))
            table[index, (size - shift - index) % size] = 1.0
            tables.append(np.kron(np.eye(256 // size), table))
    return np.concatenate(tables).astype(ml_dtypes.bfloat16)


Y_ROWS, X_ROWS, TURN_ROWS = 8 * 384, 3 * 1024, 4 * 256
X_START, TURN_START = Y_ROWS, Y_ROWS + X_ROWS
TABLE_ROWS = Y_ROWS + X_ROWS + TURN_ROWS


def plane_tables():
    return np.concatenate([y_tables(), x_tables(), turn_tables()])


def sort_table():
    index = np.arange(512)
    order = np.zeros((512, 512))
    order[index, (index % 4) * 128 + index // 4] = 1.0
    return order.astype(ml_dtypes.bfloat16)


def split(value):
    high = value.astype(BF)
    low = (value - high.astype(F32)).astype(BF)
    return high, low


def dot(left, right):
    return lax.dot_general(left, right, (((1,), (0,)), ((), ())), preferred_element_type=F32)


def dot_nt(left, right):
    return lax.dot_general(left, right, (((1,), (1,)), ((), ())), preferred_element_type=F32)


def spline_weights(fractions):
    values = [fractions, 1.0 - fractions]
    for degree in (3, 4, 5):
        updated = []
        for position in range(degree):
            term = None
            if position < degree - 1:
                term = (fractions + float(position)) * values[position]
            if position >= 1:
                lower = (float(degree - position) - fractions) * values[position - 1]
                term = lower if term is None else term + lower
            updated.append(term * (1.0 / (degree - 1)))
        values = updated
    return values


def pick(selected, weights):
    total = jnp.where(selected == 4, weights[4], 0.0)
    for degree in (3, 2, 1, 0):
        total = jnp.where(selected == degree, weights[degree], total)
    return total


def occupied_rows(count_ref, chunk):
    sub = lax.broadcasted_iota(jnp.int32, (8, 128), 0)
    slot = lax.broadcasted_iota(jnp.int32, (8, 128), 1)
    counts = jnp.zeros((8, 128), jnp.int32)
    for row in range(8):
        counts = jnp.where(sub == row, count_ref[chunk // 2, (chunk % 2) * 8 + row], counts)
    return slot < counts


def prepare(frac_ref, base_ref, wx_ref, wy_ref, wz_ref, charge_of):
    def chunk_step(chunk, carry):
        rows = pl.ds(pl.multiple_of(chunk * 8, 8), 8)
        weights = spline_weights(frac_ref[0, rows, :])
        offset = (base_ref[0, rows, :] & 3) + 4
        charge = charge_of(chunk, rows)
        for position in range(8):
            window = pick(offset - position, weights)
            wx_ref[position, rows, :] = window if charge is None else window * charge
        for degree, weight in enumerate(spline_weights(frac_ref[1, rows, :])):
            wy_ref[degree, rows, :] = weight
        for degree, weight in enumerate(spline_weights(frac_ref[2, rows, :])):
            wz_ref[degree, rows, :] = weight
        return carry

    lax.fori_loop(0, CELLS // 8, chunk_step, 0)


def depth_weights(base_ref, wz_ref, cell):
    row = pl.ds(cell, 1)
    start = (base_ref[2, row, :] - 2) & (NZ - 1)
    block, inside = start >> 5, start & 31
    weights = [wz_ref[degree, row, :] for degree in range(5)]
    level = lax.broadcasted_iota(jnp.int32, (40, 128), 0)
    window = pick(4 - (level - inside), weights)
    high = window.astype(BF).astype(F32)
    low = window - high
    parts = []
    for value in (high, low):
        pieces = []
        for index in range(8):
            here = block == index
            before = block == (index - 1) % 8
            first = jnp.where(here, value[:8], jnp.where(before, value[32:], 0.0))
            rest = jnp.where(here, value[8:32], 0.0)
            pieces += [first, rest]
        parts.append(jnp.concatenate(pieces, axis=0).astype(BF))
    return parts


def pair_depth(base_ref, wz_ref, cell):
    first = depth_weights(base_ref, wz_ref, cell)
    second = depth_weights(base_ref, wz_ref, cell + 1)
    return (
        jnp.concatenate([first[0], second[0]], axis=1),
        jnp.concatenate([first[1], second[1]], axis=1),
    )


def pair_window_y(base_ref, wy_ref, cell):
    parts = []
    for side in (0, 1):
        row = pl.ds(cell + side, 1)
        position = lax.broadcasted_iota(jnp.int32, (16, 128), 0)
        selected = ((base_ref[1, row, :] & 3) + 4 + 4 * side) - position
        parts.append(pick(selected, [wy_ref[degree, row, :] for degree in range(5)]))
    return jnp.concatenate(parts, axis=1)


def pair_row(ref, position, cell):
    return jnp.concatenate(
        [ref[position, pl.ds(cell, 1), :], ref[position, pl.ds(cell + 1, 1), :]], axis=1
    )


def start_all(moves, sems):
    copies = [
        pltpu.make_async_copy(source, target, sems.at[index])
        for index, (source, target) in enumerate(moves)
    ]
    for copy in copies:
        copy.start()
    return copies


def spread_kernel(
    count_hbm,
    cot_hbm,
    frac_hbm,
    base_hbm,
    table_hbm,
    out_hbm,
    count_ref,
    cot_ref,
    frac_ref,
    base_ref,
    table_ref,
    out_ref,
    ext_ref,
    wx_ref,
    wy_ref,
    wz_ref,
    sems,
    out_sems,
):
    copies = start_all(
        [
            (count_hbm, count_ref),
            (cot_hbm, cot_ref),
            (frac_hbm, frac_ref),
            (base_hbm, base_ref),
            (table_hbm, table_ref),
        ],
        sems,
    )

    def clear(step, carry):
        rows = pl.ds(pl.multiple_of(step * EXT_Y, 8), EXT_Y)
        for half in (0, 1):
            ext_ref[half, rows, :] = jnp.zeros((EXT_Y, 128), F32)
        return carry

    lax.fori_loop(0, EXT_X, clear, 0, unroll=4)
    for copy in copies[:4]:
        copy.wait()

    def charge_of(chunk, rows):
        return jnp.where(occupied_rows(count_ref, chunk), cot_ref[rows, :], 0.0)

    prepare(frac_ref, base_ref, wx_ref, wy_ref, wz_ref, charge_of)

    def pair_step(step, carry):
        cell_x, pair = step // 8, step % 8
        cell = step * 2
        depth_high, depth_low = pair_depth(base_ref, wz_ref, cell)
        window_y = pair_window_y(base_ref, wy_ref, cell)
        lifted = jnp.concatenate(
            [pair_row(wx_ref, u, cell) * window_y for u in range(8)], axis=0
        )
        high, low = split(lifted)
        both = dot_nt(jnp.concatenate([high, low], axis=0), depth_high)
        patch = both[:128] + both[128:] + dot_nt(high, depth_low)
        for u in range(8):
            rows = pl.ds(pl.multiple_of((cell_x * 4 + u) * EXT_Y + pair * 8, 8), 16)
            for half in (0, 1):
                ext_ref[half, rows, :] += patch[16 * u : 16 * u + 16, 128 * half : 128 * half + 128]
        return carry

    lax.fori_loop(0, CELLS // 2, pair_step, 0, unroll=8)

    lane = lax.broadcasted_iota(jnp.int32, (128, 128), 1)

    def transform(blocks, first_row):
        high, low = split(jnp.concatenate(blocks, axis=0))
        both = dot_nt(table_ref[...], high)
        planes = both[:256] + both[256:] + dot_nt(table_ref[:256], low)
        for duo in (0, 1):
            first = planes[:128, 128 * duo : 128 * duo + 128]
            second = planes[128:, 128 * duo : 128 * duo + 128]
            left = jnp.where(lane < 64, first, pltpu.roll(second, 64, 1))
            right = jnp.where(lane < 64, pltpu.roll(first, 64, 1), second)
            out_ref[pl.ds(first_row + 2 * duo, 128, stride=ROWS), :] = left
            out_ref[pl.ds(first_row + 2 * duo + 1, 128, stride=ROWS), :] = right

    def send(index):
        rows = pl.ds(8 * index, 8)
        copy = pltpu.make_async_copy(
            out_ref.reshape(DEVICES, ROWS, 128).at[:, rows, :],
            out_hbm.at[:, rows, :],
            out_sems.at[index],
        )
        copy.start()
        return copy

    copies[4].wait()
    sends = []
    for step in range(9):
        blocks = []
        for row in range(4):
            rows = pl.ds((step * 4 + row) * EXT_Y, 64)
            blocks.append(jnp.concatenate([ext_ref[0, rows, :], ext_ref[1, rows, :]], axis=1))
        transform(blocks, step * 4)
        if step % 2 == 1:
            sends.append(send(step // 2))
    blocks = []
    for rim in range(4):
        rows = pl.ds(64 + rim, EXT_X, stride=EXT_Y)
        block = jnp.concatenate([ext_ref.at[0][rows, :], ext_ref.at[1][rows, :]], axis=1)
        blocks.append(jnp.concatenate([block, jnp.zeros((24, 256), F32)], axis=0))
    transform(blocks, 36)
    sends.append(send(4))
    for copy in sends:
        copy.wait()


def sort_kernel(
    flag_ref,
    influence_hbm,
    zero_hbm,
    sort_hbm,
    tables_hbm,
    weight_hbm,
    kept_hbm,
    sort,
    influence,
    zero_plane,
    weight_ref,
    tables,
    sems,
):
    plane, middle = flag_ref[0], flag_ref[1]
    moves = [(sort_hbm, sort)]
    for part in range(4):
        columns = pl.ds(128 * part, 128)
        moves.append((influence_hbm.at[plane, :, columns], influence.at[part]))
        moves.append((zero_hbm.at[:, columns], zero_plane.at[part]))
    moves.append((tables_hbm, tables))
    copies = start_all(moves, sems)
    for copy in copies[:-1]:
        copy.wait()

    def put(first, f, value):
        high, low = split(value)
        value = dot(high, sort[...]) + dot(low, sort[...])
        for residue in range(4):
            weight_ref[first + 4 * f + residue] = value[:, 128 * residue : 128 * residue + 128]

    def plane_rows(planes, f):
        rows = pl.ds(f, 256, stride=2)
        return jnp.concatenate([planes.at[part][rows, :] for part in range(4)], axis=1)

    @pl.when(middle == 0)
    def _plain():
        for f in (0, 1):
            put(0, f, plane_rows(influence, f))
        for which in range(8):
            weight_ref[8 + which] = jnp.zeros((256, 128), F32)

    @pl.when(middle != 0)
    def _mixed():
        for f in (0, 1):
            own, other = plane_rows(influence, f), plane_rows(zero_plane, f)
            put(0, f, (own + other) * 0.5)
            put(8, f, (own - other) * 0.5)

    pltpu.sync_copy(weight_ref, weight_hbm.at[pl.ds(0, 16)])
    copies[-1].wait()
    pltpu.sync_copy(tables, kept_hbm.at[pl.ds(0, TABLE_ROWS), :])


def plane_kernel(
    flag_ref,
    in_ref,
    weight_hbm,
    tables_hbm,
    out_ref,
    weight_ref,
    tables,
    block_high,
    block_low,
    rim_high,
    rim_low,
    spectrum,
    result,
    sems,
):
    middle = flag_ref[1]

    def table_move(first, count):
        rows = pl.ds(first, count)
        return tables_hbm.at[rows, :], tables.at[rows, :]

    moves = [
        table_move(0, Y_ROWS),
        table_move(X_START, X_ROWS),
        (weight_hbm.at[pl.ds(0, 8)], weight_ref.at[pl.ds(0, 8)]),
        table_move(TURN_START, TURN_ROWS),
        (weight_hbm.at[pl.ds(8, 8)], weight_ref.at[pl.ds(8, 8)]),
    ]
    copies = [
        pltpu.make_async_copy(source, target, sems.at[index])
        for index, (source, target) in enumerate(moves)
    ]
    for copy in copies[:3]:
        copy.start()

    @pl.when(middle != 0)
    def _more():
        for copy in copies[3:]:
            copy.start()

    sub = lax.broadcasted_iota(jnp.int32, (8, 128), 0)
    turn_sign = jnp.where(lax.broadcasted_iota(jnp.int32, (32, 128), 1) < 64, -1.0, 1.0)

    def times_i(value):
        return pltpu.roll(value, 64, 1) * turn_sign[: value.shape[0]]

    def block_rows(p, q, first, count):
        return pl.ds((p * PY + q) * ROWS + first, count)

    def rim_rows(p):
        tiles = []
        for q in range(0, PY, 2):
            even = in_ref[block_rows(p, q, 32, 8), :]
            odd = in_ref[block_rows(p, q + 1, 32, 8), :]
            tiles.append(jnp.where(sub < 4, pltpu.roll(even, 4, 0), odd))
        tiles.append(jnp.zeros((96, 128), F32))
        return jnp.concatenate(tiles, axis=0).T

    def main_rows(p, q):
        own = in_ref[block_rows(p, q, 0, 32), :]
        edge = in_ref[block_rows((p + PX - 1) % PX, q, 32, 8), :]
        return jnp.concatenate([own[:8] + jnp.where(sub < 4, edge, 0.0), own[8:]], axis=0)

    turned_rims = {p: rim_rows(p) for p in (7, 15)}

    def edge_rows(p):
        before = turned_rims[(p + PX - 1) % PX]
        if p not in turned_rims:
            turned_rims[p] = rim_rows(p)
        turned = turned_rims[p]
        own = turned[0:32] + pltpu.roll(turned[64:96], 32, 1)
        edge = before[32:40] + pltpu.roll(before[96:104], 32, 1)
        first = own[:8] + jnp.where(sub < 4, edge, 0.0)
        return jnp.concatenate([first, own[8:]], axis=0)

    for p in range(8):
        rows = pl.ds(p * 32, 32)
        for q in range(2):
            columns = pl.ds(128 * q, 128)
            near = [main_rows(p, 2 * t + q) for t in range(4)]
            far = [main_rows(p + 8, 2 * t + q) for t in range(4)]
            for f, sign in ((0, 1.0), (1, -1.0)):
                a = [x + sign * y for x, y in zip(near, far)]
                sum_even, sum_odd = a[0] + a[2], a[1] + a[3]
                diff_even, diff_odd = a[0] - a[2], times_i(a[1] - a[3])
                parts = (
                    sum_even + sum_odd,
                    diff_even - diff_odd,
                    sum_even - sum_odd,
                    diff_even + diff_odd,
                )
                for residue, value in enumerate(parts):
                    high, low = split(value)
                    block_high[4 * f + residue, rows, columns] = high
                    block_low[4 * f + residue, rows, columns] = low
        near, far = edge_rows(p), edge_rows(p + 8)
        for f, value in ((0, near + far), (1, near - far)):
            rim_high[f, rows, :], rim_low[f, rows, :] = split(value)

    def y_table(residue, part):
        return tables[pl.ds((2 * residue + part) * 384, 384), :]

    def x_table(index):
        return pl.ds(X_START + 1024 * index, 1024)

    def left_products(rows, value):
        table = tables[rows, :]
        high, low = split(value)
        both = dot(table, high)
        total = both[:512] + both[512:] + dot(table[:512], low)
        return total[:256], total[256:]

    blocks = [(f, residue) for f in (0, 1) for residue in range(4)]
    copies[0].wait()
    copies[1].wait()
    for f, residue in blocks:
        which = 4 * f + residue
        high = jnp.concatenate([block_high[which], rim_high[f]], axis=1)
        low = jnp.concatenate([block_low[which], rim_low[f]], axis=1)
        both = dot(jnp.concatenate([high, low], axis=0), y_table(residue, 0))
        along_y = both[:256] + both[256:] + dot(high, y_table(residue, 1))
        cosine, sine = left_products(x_table(f), along_y)
        spectrum[which, :, :128] = cosine[:, :128] + sine[:, 128:]
        spectrum[which, :, 128:] = cosine[:, 128:] - sine[:, :128]

    copies[2].wait()

    @pl.when(middle == 0)
    def _scale():
        for which in range(8):
            for part in (0, 1):
                spectrum[which, :, pl.ds(128 * part, 128)] *= weight_ref[which]

    @pl.when(middle != 0)
    def _scale_mixed():
        copies[3].wait()
        copies[4].wait()
        for f in (0, 1):
            left = tables[pl.ds(TURN_START + 256 * f, 256), :]
            turned = []
            for residue in range(4):
                right = tables[pl.ds(TURN_START + 512 + 256 * (residue > 0), 256), :]
                high, low = split(spectrum[4 * f + (4 - residue) % 4])
                high, low = split(dot(left, high) + dot(left, low))
                turned.append(dot(high, right) + dot(low, right))
            for residue in range(4):
                which = 4 * f + residue
                for part, sign in ((0, 1.0), (1, -1.0)):
                    columns = pl.ds(128 * part, 128)
                    spectrum[which, :, columns] = (
                        spectrum[which, :, columns] * weight_ref[which]
                        + sign * turned[residue][:, 128 * part : 128 * part + 128] * weight_ref[8 + which]
                    )

    for f, residue in blocks:
        which = 4 * f + residue
        cosine, sine = left_products(x_table(2 * f), spectrum[which])
        back = jnp.concatenate(
            [cosine[:, :128] - sine[:, 128:], cosine[:, 128:] + sine[:, :128]], axis=1
        )
        high, low = split(back)
        both = dot_nt(jnp.concatenate([high, low], axis=0), y_table(residue, 0))
        result[which] = both[:256] + both[256:] + dot_nt(high, y_table(residue, 1))

    def chunk_copy(p):
        rows = pl.ds(p * PY * ROWS, PY * ROWS)
        return pltpu.make_async_copy(out_ref.at[rows, :], out_hbm.at[rows, :], out_sems.at[p])

    def quarters(first, count, columns):
        found = []
        for f in (0, 1):
            a = [result[4 * f + residue, pl.ds(first, count), columns] for residue in range(4)]
            sum_even, sum_odd = a[0] + a[2], a[1] + a[3]
            diff_even, diff_odd = a[0] - a[2], times_i(a[1] - a[3])
            found.append(
                (
                    sum_even + sum_odd,
                    diff_even + diff_odd,
                    sum_even - sum_odd,
                    diff_even - diff_odd,
                )
            )
        return found

    def total(first, count):
        rows, columns = pl.ds(first, count), pl.ds(256, 128)
        return [
            (result[4 * f, rows, columns] + result[4 * f + 1, rows, columns])
            + (result[4 * f + 2, rows, columns] + result[4 * f + 3, rows, columns])
            for f in (0, 1)
        ]

    for p in range(8):
        first, after = p * 32, ((p + 1) % 8) * 32
        wrap = -1.0 if p == 7 else 1.0
        own, edge = total(first, 32), total(after, 8)
        rims = []
        for sign in (1.0, -1.0):
            tall = jnp.concatenate(
                [own[0] + sign * own[1], edge[0] + (sign * wrap) * edge[1], jnp.zeros((88, 128), F32)],
                axis=0,
            ).T
            rims.append(tall[0:32] + pltpu.roll(tall[32:64], 64, 1))
        for q in range(2):
            columns = pl.ds(128 * q, 128)
            own, edge = quarters(first, 32, columns), quarters(after, 8, columns)
            for t in range(4):
                target_q = 2 * t + q
                for far, sign in ((0, 1.0), (8, -1.0)):
                    target_p = p + far
                    out_ref[block_rows(target_p, target_q, 0, 32), :] = own[0][t] + sign * own[1][t]
                    x_rim = edge[0][t] + (sign * wrap) * edge[1][t]
                    tile = rims[far // 8][8 * (target_q // 2) : 8 * (target_q // 2) + 8]
                    if target_q % 2 == 0:
                        tile = pltpu.roll(tile, 4, 0)
                    out_ref[block_rows(target_p, target_q, 32, 8), :] = jnp.where(
                        sub < 4, x_rim, tile
                    )


def atoms_kernel(
    frac_hbm,
    base_hbm,
    table_hbm,
    depth_ref,
    window_out,
    frac_ref,
    base_ref,
    table_ref,
    wx_ref,
    wy_ref,
    wz_ref,
    sems,
):
    step = pl.program_id(0)

    @pl.when(step == 0)
    def _first():
        moves = [(frac_hbm, frac_ref), (base_hbm, base_ref), (table_hbm, table_ref)]
        for copy in start_all(moves, sems):
            copy.wait()
        prepare(frac_ref, base_ref, wx_ref, wy_ref, wz_ref, lambda chunk, rows: None)

    def pair_step(index, carry):
        cell = step * 16 + index * 2
        high, low = pair_depth(base_ref, wz_ref, cell)
        both = dot(table_ref[...], high)
        depth_ref[index, 0], depth_ref[index, 1] = split(
            both[:256] + both[256:] + dot(table_ref[:256], low)
        )
        window_out[index, pl.ds(8, 16), :] = pair_window_y(base_ref, wy_ref, cell)
        for u in range(8):
            window_out[index, pl.ds(u, 1), :] = pair_row(wx_ref, u, cell)
        return carry

    lax.fori_loop(0, 8, pair_step, 0, unroll=2)


def gather_kernel(
    count_hbm,
    in_ref,
    depth_hbm,
    window_hbm,
    out_ref,
    count_ref,
    depth_ref,
    window_ref,
    ext_ref,
    sems,
):
    moves = [(count_hbm, count_ref), (window_hbm.at[pl.ds(0, CELLS // 2)], window_ref)]
    for row in range(8):
        pairs = pl.ds(8 * row, 8)
        moves.append((depth_hbm.at[pairs], depth_ref.at[pairs]))
    copies = start_all(moves, sems)

    def turned(row):
        block = in_ref[pl.ds(row, 128, stride=ROWS), :].T
        return block[:64], block[64:]

    def row_step(row, carry):
        rows = pl.ds(pl.multiple_of(row * EXT_Y, 8), 64)
        last = pl.ds(pl.multiple_of(row * EXT_Y + 64, 8), 8)
        first, second = turned(row)
        ext_ref[0, rows, :] = first
        ext_ref[1, rows, :] = second
        for half in (0, 1):
            ext_ref[half, last, :] = jnp.zeros((8, 128), F32)
        return carry

    lax.fori_loop(0, 36, row_step, 0, unroll=6)
    for rim in range(4):
        rows = pl.ds(64 + rim, EXT_X, stride=EXT_Y)
        first, second = turned(36 + rim)
        ext_ref.at[0][rows, :] = first[:EXT_X]
        ext_ref.at[1][rows, :] = second[:EXT_X]
    for copy in copies[:2]:
        copy.wait()

    def pair_work(cell_x, pair):
        index = cell_x * 8 + pair
        windows = []
        for u in range(8):
            rows = pl.ds(pl.multiple_of((cell_x * 4 + u) * EXT_Y + pair * 8, 8), 16)
            windows.append(jnp.concatenate([ext_ref[0, rows, :], ext_ref[1, rows, :]], axis=1))
        high, low = split(jnp.concatenate(windows, axis=0))
        both = dot(jnp.concatenate([high, low], axis=0), depth_ref[index, 0])
        part = both[:128] + both[128:] + dot(high, depth_ref[index, 1])
        total = part[:16] * window_ref[index, pl.ds(0, 1), :]
        for u in range(1, 8):
            total += part[16 * u : 16 * u + 16] * window_ref[index, pl.ds(u, 1), :]
        total = jnp.sum(total * window_ref[index, pl.ds(8, 16), :], axis=0, keepdims=True)
        out_ref[pl.ds(index * 2, 1), :] = total[:, :128]
        out_ref[pl.ds(index * 2 + 1, 1), :] = total[:, 128:]

    for cell_x in range(8):
        copies[2 + cell_x].wait()
        for pair in range(8):
            pair_work(cell_x, pair)

    def mask_step(chunk, carry):
        rows = pl.ds(pl.multiple_of(chunk * 8, 8), 8)
        out_ref[rows, :] = jnp.where(occupied_rows(count_ref, chunk), out_ref[rows, :], 0.0)
        return carry

    lax.fori_loop(0, CELLS // 8, mask_step, 0, unroll=2)


VMEM = pl.BlockSpec(memory_space=pltpu.VMEM)
SMEM = pl.BlockSpec(memory_space=pltpu.SMEM)
HBM = pl.BlockSpec(memory_space=pltpu.HBM)
MIB = 1024 * 1024


def scratch(shape, dtype=F32):
    return pltpu.VMEM(shape, dtype)


def dmas(count):
    return pltpu.SemaphoreType.DMA((count,))


def params(mib):
    return pltpu.CompilerParams(vmem_limit_bytes=mib * MIB)


def cost(flops):
    return pl.CostEstimate(flops=flops, bytes_accessed=10**7, transcendentals=0)


ATOMS = (3, CELLS, 128)
WEIGHTS = [scratch((8, CELLS, 128)), scratch((5, CELLS, 128)), scratch((5, CELLS, 128))]
EXTENDED = scratch((2, EXT_X * EXT_Y, 128))


def per_device(cotangent, fraction, grid_base, cell_count, influence):
    device = lax.axis_index("px") * PY + lax.axis_index("py")
    flags = jnp.stack([(device < MIDDLE).astype(jnp.int32), (device == MIDDLE).astype(jnp.int32)])
    zero_plane = lax.ppermute(influence[0], ("px", "py"), [(0, MIDDLE)])
    fraction = fraction.reshape(ATOMS)
    grid_base = grid_base.reshape(ATOMS)
    forward_z, inverse_z = depth_tables()

    sent = pl.pallas_call(
        spread_kernel,
        out_shape=jax.ShapeDtypeStruct((DEVICES, ROWS, 128), F32),
        in_specs=[HBM] * 5,
        out_specs=HBM,
        scratch_shapes=[
            pltpu.SMEM((8, 16), jnp.int32),
            scratch((CELLS, 128)),
            scratch(ATOMS),
            scratch(ATOMS, jnp.int32),
            scratch((512, 256), BF),
            scratch((DEVICES * ROWS, 128)),
            EXTENDED,
            *WEIGHTS,
            dmas(5),
            dmas(5),
        ],
        compiler_params=params(62),
        cost_estimate=cost(10**10),
        name="spread",
    )(cell_count, cotangent.reshape(CELLS, 128), fraction, grid_base, forward_z)

    def exchange(array):
        return lax.all_to_all(array, ("px", "py"), split_axis=0, concat_axis=0, tiled=True)

    sent, zero_plane, fraction, grid_base = lax.optimization_barrier(
        (sent, zero_plane, fraction, grid_base)
    )
    planes = exchange(sent).reshape(DEVICES * ROWS, 128)
    weight, tables = pl.pallas_call(
        sort_kernel,
        out_shape=(
            jax.ShapeDtypeStruct((136, 256, 128), F32),
            jax.ShapeDtypeStruct((34816, 256), BF),
        ),
        in_specs=[SMEM] + [HBM] * 4,
        out_specs=(HBM, HBM),
        scratch_shapes=[
            scratch((512, 512), BF),
            scratch((4, 512, 128)),
            scratch((4, 512, 128)),
            scratch((16, 256, 128)),
            scratch((TABLE_ROWS, 256), BF),
            dmas(10),
        ],
        compiler_params=params(56),
        cost_estimate=cost(10**9),
        name="sort_influence",
    )(flags, influence, zero_plane, sort_table(), plane_tables())

    pairs = CELLS // 2
    depth, window = pl.pallas_call(
        atoms_kernel,
        grid=(8,),
        out_shape=(
            jax.ShapeDtypeStruct((pairs, 2, 256, 256), BF),
            jax.ShapeDtypeStruct((704, 24, 256), F32),
        ),
        in_specs=[HBM] * 3,
        out_specs=(
            pl.BlockSpec((8, 2, 256, 256), lambda i: (i, 0, 0, 0)),
            pl.BlockSpec((8, 24, 256), lambda i: (i, 0, 0)),
        ),
        scratch_shapes=[
            scratch(ATOMS),
            scratch(ATOMS, jnp.int32),
            scratch((512, 256), BF),
            *WEIGHTS,
            dmas(3),
        ],
        compiler_params=params(56),
        cost_estimate=cost(10**10),
        name="atoms",
    )(fraction, grid_base, inverse_z)

    planes, depth, window = lax.optimization_barrier((planes, depth, window))
    back = pl.pallas_call(
        plane_kernel,
        out_shape=jax.ShapeDtypeStruct((DEVICES * ROWS, 128), F32),
        in_specs=[SMEM, VMEM, HBM, HBM],
        out_specs=VMEM,
        scratch_shapes=[
            scratch((16, 256, 128)),
            scratch((TABLE_ROWS, 256), BF),
            scratch((8, 256, 256), BF),
            scratch((8, 256, 256), BF),
            scratch((2, 256, 128), BF),
            scratch((2, 256, 128), BF),
            scratch((8, 256, 256)),
            scratch((8, 256, 384)),
            dmas(5),
        ],
        compiler_params=params(48),
        name="planes",
    )(flags, planes, weight, tables)
    returned = exchange(back.reshape(DEVICES, ROWS, 128)).reshape(DEVICES * ROWS, 128)

    gradient = pl.pallas_call(
        gather_kernel,
        out_shape=jax.ShapeDtypeStruct((CELLS, 128), F32),
        in_specs=[HBM, VMEM, HBM, HBM],
        out_specs=VMEM,
        scratch_shapes=[
            pltpu.SMEM((8, 16), jnp.int32),
            scratch((pairs, 2, 256, 256), BF),
            scratch((pairs, 24, 256)),
            EXTENDED,
            dmas(10),
        ],
        compiler_params=params(48),
        name="gather",
    )(cell_count, returned, depth, window)
    return gradient.reshape(cotangent.shape)


def solution(mesh):
    placed = (
        P("px", "py", None),
        P(None, "px", "py", None),
        P(None, "px", "py", None),
        P("px", "py"),
        P(("px", "py"), None, None),
    )
    return jax.shard_map(
        per_device, mesh=mesh, in_specs=placed, out_specs=P("px", "py", None), check_vma=False
    )
```

```python
import functools

import jax
import jax.numpy as jnp
import ml_dtypes
import numpy as np
from jax import lax
from jax.experimental import pallas as pl
from jax.experimental.pallas import tpu as pltpu
from jax.sharding import PartitionSpec as P

NX, NY, NZ = 512, 512, 256
PX, PY = 16, 8
DEVICES = PX * PY
MIDDLE = DEVICES // 2
CELLS = 128
ROWS = 40
EXT_X, EXT_Y = 40, 72
HALF_ROWS = 264
ATOM_CALLS = ((0, 2, 16), (2, 2, 16), (4, 4, 80))
ATOM_PARTS = len(ATOM_CALLS)
BF, F32 = jnp.bfloat16, jnp.float32


def split_np(table):
    high = table.astype(ml_dtypes.bfloat16)
    low = (table - high.astype(np.float64)).astype(ml_dtypes.bfloat16)
    return high, low


def depth_angles():
    device = np.arange(DEVICES)
    wave = np.where(device < MIDDLE, 2 * device + 1, 2 * device)
    return 2.0 * np.pi * ((wave[:, None] * np.arange(NZ)[None, :]) % NZ) / NZ


def depth_tables():
    angle = depth_angles()
    first, second = np.cos(angle), -np.sin(angle)
    second[MIDDLE] = 1.0
    forward = np.concatenate([first, second])
    gain = np.full((DEVICES, 1), 2.0)
    gain[MIDDLE] = 1.0
    inverse = forward * np.concatenate([gain, gain]) / (NX * NY * NZ)
    return np.concatenate(split_np(forward)), np.concatenate(split_np(inverse))


def y_tables():
    tables = []
    for residue in range(4):
        wave = 4 * np.arange(128) + residue
        main = 64 * np.arange(2)[:, None] + np.arange(64)[None, :]
        rim = (64 * (np.arange(8)[:, None] + 1) + np.arange(4)[None, :]) % NY

        def pair(position):
            angle = 2.0 * np.pi * ((position[..., None] * wave) % NY) / NY
            cosine, sine = np.cos(angle), np.sin(angle)
            first = np.concatenate([cosine, -sine], axis=-1)
            second = np.concatenate([sine, cosine], axis=-1)
            return first, second

        whole = np.stack(pair(main), axis=1).reshape(256, 256)
        edge = np.stack(pair(rim), axis=0).reshape(64, 256)
        whole = np.concatenate([whole, edge, np.zeros((64, 256))])
        tables.extend(split_np(whole))
    return np.concatenate(tables)


def x_tables():
    forward, inverse = [], []
    for parity in (0, 1):
        wave = 2 * np.arange(256) + parity
        angle = 2.0 * np.pi * ((wave[:, None] * np.arange(256)[None, :]) % NX) / NX
        cosine, sine = np.cos(angle), np.sin(angle)
        forward.append(np.concatenate(split_np(np.concatenate([cosine, sine]))))
        inverse.append(np.concatenate(split_np(np.concatenate([cosine.T, sine.T]))))
    return np.concatenate(forward + inverse[1:])


def turn_tables():
    tables = []
    for size in (256, 128):
        index = np.arange(size)
        for shift in (0, 1):
            table = np.zeros((size, size))
            table[index, (size - shift - index) % size] = 1.0
            tables.append(np.kron(np.eye(256 // size), table))
    return np.concatenate(tables).astype(ml_dtypes.bfloat16)


Y_ROWS, X_ROWS, TURN_ROWS = 8 * 384, 3 * 1024, 4 * 256
X_START, TURN_START = Y_ROWS, Y_ROWS + X_ROWS
TABLE_ROWS = Y_ROWS + X_ROWS + TURN_ROWS


def plane_tables():
    return np.concatenate([y_tables(), x_tables(), turn_tables()])


def sort_table():
    index = np.arange(512)
    order = np.zeros((512, 512))
    order[index, (index % 4) * 128 + index // 4] = 1.0
    return order.astype(ml_dtypes.bfloat16)


def split(value):
    high = value.astype(BF)
    low = (value - high.astype(F32)).astype(BF)
    return high, low


def dot(left, right):
    return lax.dot_general(left, right, (((1,), (0,)), ((), ())), preferred_element_type=F32)


def dot_nt(left, right):
    return lax.dot_general(left, right, (((1,), (1,)), ((), ())), preferred_element_type=F32)


def spline_weights(fractions):
    values = [fractions, 1.0 - fractions]
    for degree in (3, 4, 5):
        updated = []
        for position in range(degree):
            term = None
            if position < degree - 1:
                term = (fractions + float(position)) * values[position]
            if position >= 1:
                lower = (float(degree - position) - fractions) * values[position - 1]
                term = lower if term is None else term + lower
            updated.append(term * (1.0 / (degree - 1)))
        values = updated
    return values


def pick(selected, weights):
    total = jnp.where(selected == 4, weights[4], 0.0)
    for degree in (3, 2, 1, 0):
        total = jnp.where(selected == degree, weights[degree], total)
    return total


def occupied_rows(count_ref, chunk):
    sub = lax.broadcasted_iota(jnp.int32, (8, 128), 0)
    slot = lax.broadcasted_iota(jnp.int32, (8, 128), 1)
    counts = jnp.zeros((8, 128), jnp.int32)
    for row in range(8):
        counts = jnp.where(sub == row, count_ref[chunk // 2, (chunk % 2) * 8 + row], counts)
    return slot < counts


def prepare(frac_ref, base_ref, wx_ref, wy_ref, wz_ref, charge_of):
    def chunk_step(chunk, carry):
        rows = pl.ds(pl.multiple_of(chunk * 8, 8), 8)
        weights = spline_weights(frac_ref[0, rows, :])
        offset = (base_ref[0, rows, :] & 3) + 4
        charge = charge_of(chunk, rows)
        for position in range(8):
            window = pick(offset - position, weights)
            wx_ref[position, rows, :] = window if charge is None else window * charge
        for degree, weight in enumerate(spline_weights(frac_ref[1, rows, :])):
            wy_ref[degree, rows, :] = weight
        for degree, weight in enumerate(spline_weights(frac_ref[2, rows, :])):
            wz_ref[degree, rows, :] = weight
        return carry

    lax.fori_loop(0, CELLS // 8, chunk_step, 0)


def cell_rows(ref, index, cell_x, cell_y):
    first = pl.multiple_of(cell_x * 16 + cell_y // 8 * 8, 8)
    return ref[index, pl.ds(first, 8), :][cell_y % 8 : cell_y % 8 + 1]


def depth_weights(base_ref, wz_ref, cell_x, cell_y):
    start = jnp.broadcast_to((cell_rows(base_ref, 2, cell_x, cell_y) - 2) & (NZ - 1), (8, 128))
    block, inside = start >> 5, start & 31
    weights = [
        jnp.broadcast_to(cell_rows(wz_ref, degree, cell_x, cell_y), (8, 128)) for degree in range(5)
    ]
    first = 4 + inside - lax.broadcasted_iota(jnp.int32, (8, 128), 0)
    highs, lows = [], []
    for step in range(5):
        window = pick(first - 8 * step, weights)
        high = window.astype(BF).astype(F32)
        highs.append(high)
        lows.append(window - high)
    parts = []
    zero = jnp.zeros((8, 128), F32)
    packed = []
    for value in (highs, lows):
        packed.append(
            [
                jnp.concatenate([value[0], value[1]], axis=0).astype(BF),
                jnp.concatenate([value[2], value[3]], axis=0).astype(BF),
                jnp.concatenate([value[4], zero], axis=0).astype(BF),
            ]
        )
    one = jnp.ones((8, 128), F32)
    hot = []
    for index in range(8):
        mark = jnp.where(block == index, one, 0.0)
        hot.append(jnp.concatenate([mark, mark], axis=0).astype(BF))
    for value in packed:
        pieces = []
        for index in range(8):
            pieces.append(value[0] * hot[index] + value[2] * hot[(index - 1) % 8])
            pieces.append(value[1] * hot[index])
        parts.append(jnp.concatenate(pieces, axis=0))
    return parts


def pair_depth(base_ref, wz_ref, cell_x, pair):
    first = depth_weights(base_ref, wz_ref, cell_x, 2 * pair)
    second = depth_weights(base_ref, wz_ref, cell_x, 2 * pair + 1)
    return (
        jnp.concatenate([first[0], second[0]], axis=1),
        jnp.concatenate([first[1], second[1]], axis=1),
    )


def pair_window_y(base_ref, wy_ref, cell_x, pair):
    parts = []
    for side in (0, 1):
        cell_y = 2 * pair + side
        position = lax.broadcasted_iota(jnp.int32, (16, 128), 0)
        selected = ((cell_rows(base_ref, 1, cell_x, cell_y) & 3) + 4 + 4 * side) - position
        weights = [cell_rows(wy_ref, degree, cell_x, cell_y) for degree in range(5)]
        parts.append(pick(selected, weights))
    return jnp.concatenate(parts, axis=1)


def pair_row(ref, position, cell_x, pair):
    return jnp.concatenate(
        [cell_rows(ref, position, cell_x, 2 * pair + side) for side in (0, 1)], axis=1
    )


def start_all(moves, sems):
    copies = [
        pltpu.make_async_copy(source, target, sems.at[index])
        for index, (source, target) in enumerate(moves)
    ]
    for copy in copies:
        copy.start()
    return copies


def spread_kernel(
    count_hbm,
    cot_hbm,
    frac_hbm,
    base_hbm,
    table_hbm,
    out_hbm,
    count_ref,
    cot_ref,
    frac_ref,
    base_ref,
    table_ref,
    out_ref,
    ext_ref,
    wx_ref,
    wy_ref,
    wz_ref,
    sems,
    out_sems,
):
    copies = start_all(
        [
            (count_hbm, count_ref),
            (cot_hbm, cot_ref),
            (frac_hbm, frac_ref),
            (base_hbm, base_ref),
            (table_hbm, table_ref),
        ],
        sems,
    )

    def clear(step, carry):
        rows = pl.ds(pl.multiple_of(step * EXT_Y, 8), EXT_Y)
        for half in (0, 1):
            ext_ref[half, rows, :] = jnp.zeros((EXT_Y, 128), F32)
        return carry

    lax.fori_loop(0, EXT_X, clear, 0, unroll=4)
    for copy in copies[:4]:
        copy.wait()

    def charge_of(chunk, rows):
        return jnp.where(occupied_rows(count_ref, chunk), cot_ref[rows, :], 0.0)

    prepare(frac_ref, base_ref, wx_ref, wy_ref, wz_ref, charge_of)

    def pair_work(cell_x, pair):
        depth_high, depth_low = pair_depth(base_ref, wz_ref, cell_x, pair)
        window_y = pair_window_y(base_ref, wy_ref, cell_x, pair)
        lifted = jnp.concatenate(
            [pair_row(wx_ref, u, cell_x, pair) * window_y for u in range(8)], axis=0
        )
        high, low = split(lifted)
        both = dot_nt(jnp.concatenate([high, low], axis=0), depth_high)
        patch = both[:128] + both[128:] + dot_nt(high, depth_low)
        for u in range(8):
            rows = pl.ds(pl.multiple_of((cell_x * 4 + u) * EXT_Y + pair * 8, 8), 16)
            for half in (0, 1):
                ext_ref[half, rows, :] += patch[16 * u : 16 * u + 16, 128 * half : 128 * half + 128]

    def cell_step(cell_x, carry):
        for pair in range(8):
            pair_work(cell_x, pair)
        return carry

    lax.fori_loop(0, 8, cell_step, 0)

    lane = lax.broadcasted_iota(jnp.int32, (128, 128), 1)

    def transform(blocks, first_row):
        high, low = split(jnp.concatenate(blocks, axis=0))
        both = dot_nt(table_ref[...], high)
        planes = both[:256] + both[256:] + dot_nt(table_ref[:256], low)
        for duo in (0, 1):
            first = planes[:128, 128 * duo : 128 * duo + 128]
            second = planes[128:, 128 * duo : 128 * duo + 128]
            left = jnp.where(lane < 64, first, pltpu.roll(second, 64, 1))
            right = jnp.where(lane < 64, pltpu.roll(first, 64, 1), second)
            out_ref[pl.ds(first_row + 2 * duo, 128, stride=ROWS), :] = left
            out_ref[pl.ds(first_row + 2 * duo + 1, 128, stride=ROWS), :] = right

    def send(index):
        rows = pl.ds(8 * index, 8)
        copy = pltpu.make_async_copy(
            out_ref.reshape(DEVICES, ROWS, 128).at[:, rows, :],
            out_hbm.at[:, rows, :],
            out_sems.at[index],
        )
        copy.start()
        return copy

    copies[4].wait()
    sends = []
    for step in range(9):
        blocks = []
        for row in range(4):
            rows = pl.ds((step * 4 + row) * EXT_Y, 64)
            blocks.append(jnp.concatenate([ext_ref[0, rows, :], ext_ref[1, rows, :]], axis=1))
        transform(blocks, step * 4)
        if step % 2 == 1:
            sends.append(send(step // 2))
    blocks = []
    for rim in range(4):
        rows = pl.ds(64 + rim, EXT_X, stride=EXT_Y)
        block = jnp.concatenate([ext_ref.at[0][rows, :], ext_ref.at[1][rows, :]], axis=1)
        blocks.append(jnp.concatenate([block, jnp.zeros((24, 256), F32)], axis=0))
    transform(blocks, 36)
    sends.append(send(4))
    for copy in sends:
        copy.wait()


def sort_kernel(
    flag_ref,
    influence_hbm,
    zero_hbm,
    sort_hbm,
    tables_hbm,
    weight_hbm,
    kept_hbm,
    sort,
    influence,
    zero_plane,
    weight_ref,
    tables,
    sems,
):
    plane, middle = flag_ref[0], flag_ref[1]
    moves = [(sort_hbm, sort)]
    for part in range(4):
        columns = pl.ds(128 * part, 128)
        moves.append((influence_hbm.at[plane, :, columns], influence.at[part]))
        moves.append((zero_hbm.at[:, columns], zero_plane.at[part, pl.ds(0, HALF_ROWS), :]))
    moves.append((tables_hbm, tables))
    copies = start_all(moves, sems)
    for copy in copies:
        copy.wait()

    def sorted_rows(planes, f, count):
        rows = pl.ds(f, 256, stride=2)
        value = jnp.concatenate([planes.at[part][rows, :] for part in range(4)], axis=1)
        if count < 256:
            value = jnp.where(lax.broadcasted_iota(jnp.int32, value.shape, 0) < count, value, 0.0)
        high, low = split(value)
        return dot(high, sort[...]) + dot(low, sort[...])

    @pl.when(middle == 0)
    def _plain():
        for f in (0, 1):
            own = sorted_rows(influence, f, 256)
            for residue in range(4):
                weight_ref[4 * f + residue] = own[:, 128 * residue : 128 * residue + 128]
        for which in range(8):
            weight_ref[8 + which] = jnp.zeros((256, 128), F32)

    @pl.when(middle != 0)
    def _mixed():
        index = lax.broadcasted_iota(jnp.int32, (256, 128), 0)
        for f in (0, 1):
            own = sorted_rows(influence, f, 256)
            half = sorted_rows(zero_plane, f, HALF_ROWS // 2)
            left = tables[pl.ds(TURN_START + 256 * f, 256), :]
            high, low = split(half)
            high, low = split(dot(left, high) + dot(left, low))
            for residue in range(4):
                which = 4 * f + residue
                columns = slice(128 * residue, 128 * residue + 128)
                other = (4 - residue) % 4
                partner = slice(128 * other, 128 * other + 128)
                right = tables[pl.ds(TURN_START + 512 + 256 * (residue > 0), 128), :][:, :128]
                turned = dot(high[:, partner], right) + dot(low[:, partner], right)
                whole = jnp.where(index <= 128 - f, half[:, columns], turned)
                weight_ref[which] = (own[:, columns] + whole) * 0.5
                weight_ref[8 + which] = (own[:, columns] - whole) * 0.5

    pltpu.sync_copy(weight_ref, weight_hbm.at[pl.ds(0, 16)])
    pltpu.sync_copy(tables, kept_hbm.at[pl.ds(0, TABLE_ROWS), :])


def plane_kernel(
    flag_ref,
    in_ref,
    weight_hbm,
    tables_hbm,
    out_ref,
    weight_ref,
    tables,
    block_high,
    block_low,
    rim_high,
    rim_low,
    spectrum,
    result,
    sems,
):
    middle = flag_ref[1]

    def table_move(first, count):
        rows = pl.ds(first, count)
        return tables_hbm.at[rows, :], tables.at[rows, :]

    moves = [
        table_move(0, Y_ROWS),
        table_move(X_START, X_ROWS),
        (weight_hbm.at[pl.ds(0, 8)], weight_ref.at[pl.ds(0, 8)]),
        table_move(TURN_START, TURN_ROWS),
        (weight_hbm.at[pl.ds(8, 8)], weight_ref.at[pl.ds(8, 8)]),
    ]
    copies = [
        pltpu.make_async_copy(source, target, sems.at[index])
        for index, (source, target) in enumerate(moves)
    ]
    for copy in copies[:3]:
        copy.start()

    @pl.when(middle != 0)
    def _more():
        for copy in copies[3:]:
            copy.start()

    sub = lax.broadcasted_iota(jnp.int32, (8, 128), 0)
    turn_sign = jnp.where(lax.broadcasted_iota(jnp.int32, (32, 128), 1) < 64, -1.0, 1.0)

    def times_i(value):
        return pltpu.roll(value, 64, 1) * turn_sign[: value.shape[0]]

    def block_rows(p, q, first, count):
        return pl.ds((p * PY + q) * ROWS + first, count)

    def rim_rows(p):
        tiles = []
        for q in range(0, PY, 2):
            even = in_ref[block_rows(p, q, 32, 8), :]
            odd = in_ref[block_rows(p, q + 1, 32, 8), :]
            tiles.append(jnp.where(sub < 4, pltpu.roll(even, 4, 0), odd))
        tiles.append(jnp.zeros((96, 128), F32))
        return jnp.concatenate(tiles, axis=0).T

    def main_rows(p, q):
        own = in_ref[block_rows(p, q, 0, 32), :]
        edge = in_ref[block_rows((p + PX - 1) % PX, q, 32, 8), :]
        return jnp.concatenate([own[:8] + jnp.where(sub < 4, edge, 0.0), own[8:]], axis=0)

    turned_rims = {p: rim_rows(p) for p in (7, 15)}

    def edge_rows(p):
        before = turned_rims[(p + PX - 1) % PX]
        if p not in turned_rims:
            turned_rims[p] = rim_rows(p)
        turned = turned_rims[p]
        own = turned[0:32] + pltpu.roll(turned[64:96], 32, 1)
        edge = before[32:40] + pltpu.roll(before[96:104], 32, 1)
        first = own[:8] + jnp.where(sub < 4, edge, 0.0)
        return jnp.concatenate([first, own[8:]], axis=0)

    for p in range(8):
        rows = pl.ds(p * 32, 32)
        for q in range(2):
            columns = pl.ds(128 * q, 128)
            near = [main_rows(p, 2 * t + q) for t in range(4)]
            far = [main_rows(p + 8, 2 * t + q) for t in range(4)]
            for f, sign in ((0, 1.0), (1, -1.0)):
                a = [x + sign * y for x, y in zip(near, far)]
                sum_even, sum_odd = a[0] + a[2], a[1] + a[3]
                diff_even, diff_odd = a[0] - a[2], times_i(a[1] - a[3])
                parts = (
                    sum_even + sum_odd,
                    diff_even - diff_odd,
                    sum_even - sum_odd,
                    diff_even + diff_odd,
                )
                for residue, value in enumerate(parts):
                    high, low = split(value)
                    block_high[4 * f + residue, rows, columns] = high
                    block_low[4 * f + residue, rows, columns] = low
        near, far = edge_rows(p), edge_rows(p + 8)
        for f, value in ((0, near + far), (1, near - far)):
            rim_high[f, rows, :], rim_low[f, rows, :] = split(value)

    def y_table(residue, part):
        return tables[pl.ds((2 * residue + part) * 384, 384), :]

    def x_table(index):
        return pl.ds(X_START + 1024 * index, 1024)

    def left_products(rows, value):
        table = tables[rows, :]
        high, low = split(value)
        both = dot(table, high)
        total = both[:512] + both[512:] + dot(table[:512], low)
        return total[:256], total[256:]

    blocks = [(f, residue) for f in (0, 1) for residue in range(4)]
    copies[0].wait()
    copies[1].wait()
    for f, residue in blocks:
        which = 4 * f + residue
        high = jnp.concatenate([block_high[which], rim_high[f]], axis=1)
        low = jnp.concatenate([block_low[which], rim_low[f]], axis=1)
        both = dot(jnp.concatenate([high, low], axis=0), y_table(residue, 0))
        along_y = both[:256] + both[256:] + dot(high, y_table(residue, 1))
        cosine, sine = left_products(x_table(f), along_y)
        spectrum[which, :, :128] = cosine[:, :128] + sine[:, 128:]
        spectrum[which, :, 128:] = cosine[:, 128:] - sine[:, :128]

    copies[2].wait()

    @pl.when(middle == 0)
    def _scale():
        for which in range(8):
            for part in (0, 1):
                spectrum[which, :, pl.ds(128 * part, 128)] *= weight_ref[which]

    @pl.when(middle != 0)
    def _scale_mixed():
        copies[3].wait()
        copies[4].wait()
        for f in (0, 1):
            left = tables[pl.ds(TURN_START + 256 * f, 256), :]
            turned = []
            for residue in range(4):
                right = tables[pl.ds(TURN_START + 512 + 256 * (residue > 0), 256), :]
                high, low = split(spectrum[4 * f + (4 - residue) % 4])
                high, low = split(dot(left, high) + dot(left, low))
                turned.append(dot(high, right) + dot(low, right))
            for residue in range(4):
                which = 4 * f + residue
                for part, sign in ((0, 1.0), (1, -1.0)):
                    columns = pl.ds(128 * part, 128)
                    spectrum[which, :, columns] = (
                        spectrum[which, :, columns] * weight_ref[which]
                        + sign * turned[residue][:, 128 * part : 128 * part + 128] * weight_ref[8 + which]
                    )

    for f, residue in blocks:
        which = 4 * f + residue
        cosine, sine = left_products(x_table(2 * f), spectrum[which])
        back = jnp.concatenate(
            [cosine[:, :128] - sine[:, 128:], cosine[:, 128:] + sine[:, :128]], axis=1
        )
        high, low = split(back)
        both = dot_nt(jnp.concatenate([high, low], axis=0), y_table(residue, 0))
        result[which] = both[:256] + both[256:] + dot_nt(high, y_table(residue, 1))

    def chunk_copy(p):
        rows = pl.ds(p * PY * ROWS, PY * ROWS)
        return pltpu.make_async_copy(out_ref.at[rows, :], out_hbm.at[rows, :], out_sems.at[p])

    def quarters(first, count, columns):
        found = []
        for f in (0, 1):
            a = [result[4 * f + residue, pl.ds(first, count), columns] for residue in range(4)]
            sum_even, sum_odd = a[0] + a[2], a[1] + a[3]
            diff_even, diff_odd = a[0] - a[2], times_i(a[1] - a[3])
            found.append(
                (
                    sum_even + sum_odd,
                    diff_even + diff_odd,
                    sum_even - sum_odd,
                    diff_even - diff_odd,
                )
            )
        return found

    def total(first, count):
        rows, columns = pl.ds(first, count), pl.ds(256, 128)
        return [
            (result[4 * f, rows, columns] + result[4 * f + 1, rows, columns])
            + (result[4 * f + 2, rows, columns] + result[4 * f + 3, rows, columns])
            for f in (0, 1)
        ]

    for p in range(8):
        first, after = p * 32, ((p + 1) % 8) * 32
        wrap = -1.0 if p == 7 else 1.0
        own, edge = total(first, 32), total(after, 8)
        rims = []
        for sign in (1.0, -1.0):
            tall = jnp.concatenate(
                [own[0] + sign * own[1], edge[0] + (sign * wrap) * edge[1], jnp.zeros((88, 128), F32)],
                axis=0,
            ).T
            rims.append(tall[0:32] + pltpu.roll(tall[32:64], 64, 1))
        for q in range(2):
            columns = pl.ds(128 * q, 128)
            own, edge = quarters(first, 32, columns), quarters(after, 8, columns)
            for t in range(4):
                target_q = 2 * t + q
                for far, sign in ((0, 1.0), (8, -1.0)):
                    target_p = p + far
                    out_ref[block_rows(target_p, target_q, 0, 32), :] = own[0][t] + sign * own[1][t]
                    x_rim = edge[0][t] + (sign * wrap) * edge[1][t]
                    tile = rims[far // 8][8 * (target_q // 2) : 8 * (target_q // 2) + 8]
                    if target_q % 2 == 0:
                        tile = pltpu.roll(tile, 4, 0)
                    out_ref[block_rows(target_p, target_q, 32, 8), :] = jnp.where(
                        sub < 4, x_rim, tile
                    )


def atoms_kernel(
    first_step,
    frac_hbm,
    base_hbm,
    table_hbm,
    depth_ref,
    window_out,
    frac_ref,
    base_ref,
    table_ref,
    wx_ref,
    wy_ref,
    wz_ref,
    sems,
):
    step = pl.program_id(0) + first_step

    @pl.when(step == first_step)
    def _first():
        moves = [(frac_hbm, frac_ref), (base_hbm, base_ref), (table_hbm, table_ref)]
        for copy in start_all(moves, sems):
            copy.wait()
        prepare(frac_ref, base_ref, wx_ref, wy_ref, wz_ref, lambda chunk, rows: None)

    for index in range(8):
        high, low = pair_depth(base_ref, wz_ref, step, index)
        both = dot(table_ref[...], high)
        depth_ref[index, 0], depth_ref[index, 1] = split(
            both[:256] + both[256:] + dot(table_ref[:256], low)
        )
        window_out[index, pl.ds(8, 16), :] = pair_window_y(base_ref, wy_ref, step, index)
        for u in range(8):
            window_out[index, pl.ds(u, 1), :] = pair_row(wx_ref, u, step, index)


def gather_kernel(
    count_hbm,
    in_ref,
    *refs,
):
    depth_refs, window_refs = refs[:ATOM_PARTS], refs[ATOM_PARTS : 2 * ATOM_PARTS]
    out_ref, count_ref, late_ref, ext_ref, sems = refs[2 * ATOM_PARTS :]
    moves = [(count_hbm, count_ref)]
    for row in range(4):
        late = pl.ds(8 * row, 8)
        moves.append((depth_refs[-1].at[late], late_ref.at[late]))
    copies = start_all(moves, sems)
    depth_refs = (*depth_refs[:-1], late_ref)

    def turned(row):
        block = in_ref[pl.ds(row, 128, stride=ROWS), :].T
        return block[:64], block[64:]

    def row_step(row, carry):
        rows = pl.ds(pl.multiple_of(row * EXT_Y, 8), 64)
        last = pl.ds(pl.multiple_of(row * EXT_Y + 64, 8), 8)
        first, second = turned(row)
        ext_ref[0, rows, :] = first
        ext_ref[1, rows, :] = second
        for half in (0, 1):
            ext_ref[half, last, :] = jnp.zeros((8, 128), F32)
        return carry

    lax.fori_loop(0, 36, row_step, 0, unroll=6)
    for rim in range(4):
        rows = pl.ds(64 + rim, EXT_X, stride=EXT_Y)
        first, second = turned(36 + rim)
        ext_ref.at[0][rows, :] = first[:EXT_X]
        ext_ref.at[1][rows, :] = second[:EXT_X]
    copies[0].wait()

    def pair_work(cell_x, pair):
        index = cell_x * 8 + pair
        part = min(cell_x // 2, 2)
        depth_ref, window_ref = depth_refs[part], window_refs[part]
        inner = index - 16 * part
        windows = []
        for u in range(8):
            rows = pl.ds(pl.multiple_of((cell_x * 4 + u) * EXT_Y + pair * 8, 8), 16)
            windows.append(jnp.concatenate([ext_ref[0, rows, :], ext_ref[1, rows, :]], axis=1))
        high, low = split(jnp.concatenate(windows, axis=0))
        both = dot(jnp.concatenate([high, low], axis=0), depth_ref[inner, 0])
        patch = both[:128] + both[128:] + dot(high, depth_ref[inner, 1])
        total = patch[:16] * window_ref[inner, pl.ds(0, 1), :]
        for u in range(1, 8):
            total += patch[16 * u : 16 * u + 16] * window_ref[inner, pl.ds(u, 1), :]
        total = jnp.sum(total * window_ref[inner, pl.ds(8, 16), :], axis=0, keepdims=True)
        out_ref[pl.ds(index * 2, 1), :] = total[:, :128]
        out_ref[pl.ds(index * 2 + 1, 1), :] = total[:, 128:]

    for cell_x in range(8):
        if cell_x >= 4:
            copies[cell_x - 3].wait()
        for pair in range(8):
            pair_work(cell_x, pair)

    def mask_step(chunk, carry):
        rows = pl.ds(pl.multiple_of(chunk * 8, 8), 8)
        out_ref[rows, :] = jnp.where(occupied_rows(count_ref, chunk), out_ref[rows, :], 0.0)
        return carry

    lax.fori_loop(0, CELLS // 8, mask_step, 0, unroll=2)


VMEM = pl.BlockSpec(memory_space=pltpu.VMEM)
SMEM = pl.BlockSpec(memory_space=pltpu.SMEM)
HBM = pl.BlockSpec(memory_space=pltpu.HBM)
MIB = 1024 * 1024


def scratch(shape, dtype=F32):
    return pltpu.VMEM(shape, dtype)


def dmas(count):
    return pltpu.SemaphoreType.DMA((count,))


def params(mib):
    return pltpu.CompilerParams(vmem_limit_bytes=mib * MIB)


def cost(flops):
    return pl.CostEstimate(flops=flops, bytes_accessed=10**7, transcendentals=0)


ATOMS = (3, CELLS, 128)
WEIGHTS = [scratch((8, CELLS, 128)), scratch((5, CELLS, 128)), scratch((5, CELLS, 128))]
EXTENDED = scratch((2, EXT_X * EXT_Y, 128))


def per_device(cotangent, fraction, grid_base, cell_count, influence):
    device = lax.axis_index("px") * PY + lax.axis_index("py")
    flags = jnp.stack([(device < MIDDLE).astype(jnp.int32), (device == MIDDLE).astype(jnp.int32)])
    zero_plane = lax.ppermute(influence[0, :HALF_ROWS], ("px", "py"), [(0, MIDDLE)])
    fraction = fraction.reshape(ATOMS)
    grid_base = grid_base.reshape(ATOMS)
    forward_z, inverse_z = depth_tables()

    sent = pl.pallas_call(
        spread_kernel,
        out_shape=jax.ShapeDtypeStruct((DEVICES, ROWS, 128), F32),
        in_specs=[HBM] * 5,
        out_specs=HBM,
        scratch_shapes=[
            pltpu.SMEM((8, 16), jnp.int32),
            scratch((CELLS, 128)),
            scratch(ATOMS),
            scratch(ATOMS, jnp.int32),
            scratch((512, 256), BF),
            scratch((DEVICES * ROWS, 128)),
            EXTENDED,
            *WEIGHTS,
            dmas(5),
            dmas(5),
        ],
        compiler_params=params(62),
        cost_estimate=cost(10**10),
        name="spread",
    )(cell_count, cotangent.reshape(CELLS, 128), fraction, grid_base, forward_z)

    def exchange(array):
        return lax.all_to_all(array, ("px", "py"), split_axis=0, concat_axis=0, tiled=True)

    sent, zero_plane, fraction, grid_base = lax.optimization_barrier(
        (sent, zero_plane, fraction, grid_base)
    )
    planes = exchange(sent).reshape(DEVICES * ROWS, 128)
    weight, tables = pl.pallas_call(
        sort_kernel,
        out_shape=(
            jax.ShapeDtypeStruct((136, 256, 128), F32),
            jax.ShapeDtypeStruct((34816, 256), BF),
        ),
        in_specs=[SMEM] + [HBM] * 4,
        out_specs=(HBM, HBM),
        scratch_shapes=[
            scratch((512, 512), BF),
            scratch((4, 512, 128)),
            scratch((4, 512, 128)),
            scratch((16, 256, 128)),
            scratch((TABLE_ROWS, 256), BF),
            dmas(10),
        ],
        compiler_params=params(56),
        cost_estimate=cost(10**9),
        name="sort_influence",
    )(flags, influence, zero_plane, sort_table(), plane_tables())

    pairs = CELLS // 2
    depths, windows = [], []
    for first_step, steps, room in ATOM_CALLS:
        depth, window = pl.pallas_call(
            functools.partial(atoms_kernel, first_step),
            grid=(steps,),
            out_shape=(
                jax.ShapeDtypeStruct((room, 2, 256, 256), BF),
                jax.ShapeDtypeStruct((8 * steps, 24, 256), F32),
            ),
            in_specs=[HBM] * 3,
            out_specs=(
                pl.BlockSpec((8, 2, 256, 256), lambda i: (i, 0, 0, 0)),
                pl.BlockSpec((8, 24, 256), lambda i: (i, 0, 0)),
            ),
            scratch_shapes=[
                scratch(ATOMS),
                scratch(ATOMS, jnp.int32),
                scratch((512, 256), BF),
                *WEIGHTS,
                dmas(3),
            ],
            compiler_params=params(60),
            cost_estimate=cost(3 * 10**9),
            name="atoms",
        )(fraction, grid_base, inverse_z)
        depths.append(depth)
        windows.append(window)

    planes, depths, windows = lax.optimization_barrier((planes, depths, windows))
    back = pl.pallas_call(
        plane_kernel,
        out_shape=jax.ShapeDtypeStruct((DEVICES * ROWS, 128), F32),
        in_specs=[SMEM, VMEM, HBM, HBM],
        out_specs=VMEM,
        scratch_shapes=[
            scratch((16, 256, 128)),
            scratch((TABLE_ROWS, 256), BF),
            scratch((8, 256, 256), BF),
            scratch((8, 256, 256), BF),
            scratch((2, 256, 128), BF),
            scratch((2, 256, 128), BF),
            scratch((8, 256, 256)),
            scratch((8, 256, 384)),
            dmas(5),
        ],
        compiler_params=params(48),
        name="planes",
    )(flags, planes, weight, tables)
    returned = exchange(back.reshape(DEVICES, ROWS, 128)).reshape(DEVICES * ROWS, 128)

    gradient = pl.pallas_call(
        gather_kernel,
        out_shape=jax.ShapeDtypeStruct((CELLS, 128), F32),
        in_specs=[HBM] + [VMEM] * ATOM_PARTS + [HBM] + [VMEM] * ATOM_PARTS,
        out_specs=VMEM,
        scratch_shapes=[
            pltpu.SMEM((8, 16), jnp.int32),
            scratch((pairs // 2, 2, 256, 256), BF),
            EXTENDED,
            dmas(5),
        ],
        compiler_params=params(40),
        name="gather",
    )(cell_count, returned, *depths, *windows)
    return gradient.reshape(cotangent.shape)


def solution(mesh):
    placed = (
        P("px", "py", None),
        P(None, "px", "py", None),
        P(None, "px", "py", None),
        P("px", "py"),
        P(("px", "py"), None, None),
    )
    return jax.shard_map(
        per_device, mesh=mesh, in_specs=placed, out_specs=P("px", "py", None), check_vma=False
    )
```

```python
import functools

import jax
import jax.numpy as jnp
import ml_dtypes
import numpy as np
from jax import lax
from jax.experimental import pallas as pl
from jax.experimental.pallas import tpu as pltpu
from jax.sharding import PartitionSpec as P

NX, NY, NZ = 512, 512, 256
PX, PY = 16, 8
DEVICES = PX * PY
MIDDLE = DEVICES // 2
CELLS = 128
ROWS = 40
EXT_X, EXT_Y = 40, 72
HALF_ROWS = 264
ATOM_CALLS = ((0, 2, 16), (2, 2, 16), (4, 4, 80))
ATOM_PARTS = len(ATOM_CALLS)
BF, F32 = jnp.bfloat16, jnp.float32


def split_np(table):
    high = table.astype(ml_dtypes.bfloat16)
    low = (table - high.astype(np.float64)).astype(ml_dtypes.bfloat16)
    return high, low


def depth_angles():
    device = np.arange(DEVICES)
    wave = np.where(device < MIDDLE, 2 * device + 1, 2 * device)
    return 2.0 * np.pi * ((wave[:, None] * np.arange(NZ)[None, :]) % NZ) / NZ


def depth_tables():
    angle = depth_angles()
    first, second = np.cos(angle), -np.sin(angle)
    second[MIDDLE] = 1.0
    forward = np.concatenate([first, second])
    gain = np.full((DEVICES, 1), 2.0)
    gain[MIDDLE] = 1.0
    inverse = forward * np.concatenate([gain, gain]) / (NX * NY * NZ)
    return np.concatenate(split_np(forward)), np.concatenate(split_np(inverse))


def y_tables():
    tables = []
    for residue in range(4):
        wave = 4 * np.arange(128) + residue
        main = 64 * np.arange(2)[:, None] + np.arange(64)[None, :]
        rim = (64 * (np.arange(8)[:, None] + 1) + np.arange(4)[None, :]) % NY

        def pair(position):
            angle = 2.0 * np.pi * ((position[..., None] * wave) % NY) / NY
            cosine, sine = np.cos(angle), np.sin(angle)
            first = np.concatenate([cosine, -sine], axis=-1)
            second = np.concatenate([sine, cosine], axis=-1)
            return first, second

        whole = np.stack(pair(main), axis=1).reshape(256, 256)
        edge = np.stack(pair(rim), axis=0).reshape(64, 256)
        whole = np.concatenate([whole, edge, np.zeros((64, 256))])
        tables.extend(split_np(whole))
    return np.concatenate(tables)


def x_tables():
    forward, inverse = [], []
    for parity in (0, 1):
        wave = 2 * np.arange(256) + parity
        angle = 2.0 * np.pi * ((wave[:, None] * np.arange(256)[None, :]) % NX) / NX
        cosine, sine = np.cos(angle), np.sin(angle)
        forward.append(np.concatenate(split_np(np.concatenate([cosine, sine]))))
        inverse.append(np.concatenate(split_np(np.concatenate([cosine.T, sine.T]))))
    return np.concatenate(forward + inverse[1:])


def turn_tables():
    tables = []
    for size in (256, 128):
        index = np.arange(size)
        for shift in (0, 1):
            table = np.zeros((size, size))
            table[index, (size - shift - index) % size] = 1.0
            tables.append(np.kron(np.eye(256 // size), table))
    return np.concatenate(tables).astype(ml_dtypes.bfloat16)


Y_ROWS, X_ROWS, TURN_ROWS = 8 * 384, 3 * 1024, 4 * 256
X_START, TURN_START = Y_ROWS, Y_ROWS + X_ROWS
TABLE_ROWS = Y_ROWS + X_ROWS + TURN_ROWS


def plane_tables():
    return np.concatenate([y_tables(), x_tables(), turn_tables()])


def sort_table():
    index = np.arange(512)
    order = np.zeros((512, 512))
    order[index, (index % 4) * 128 + index // 4] = 1.0
    return order.astype(ml_dtypes.bfloat16)


def split(value):
    high = value.astype(BF)
    low = (value - high.astype(F32)).astype(BF)
    return high, low


def dot(left, right):
    return lax.dot_general(left, right, (((1,), (0,)), ((), ())), preferred_element_type=F32)


def dot_nt(left, right):
    return lax.dot_general(left, right, (((1,), (1,)), ((), ())), preferred_element_type=F32)


def spline_weights(fractions):
    values = [fractions, 1.0 - fractions]
    for degree in (3, 4, 5):
        updated = []
        for position in range(degree):
            term = None
            if position < degree - 1:
                term = (fractions + float(position)) * values[position]
            if position >= 1:
                lower = (float(degree - position) - fractions) * values[position - 1]
                term = lower if term is None else term + lower
            updated.append(term * (1.0 / (degree - 1)))
        values = updated
    return values


def pick(selected, weights):
    total = jnp.where(selected == 4, weights[4], 0.0)
    for degree in (3, 2, 1, 0):
        total = jnp.where(selected == degree, weights[degree], total)
    return total


def occupied_rows(count_ref, chunk):
    sub = lax.broadcasted_iota(jnp.int32, (8, 128), 0)
    slot = lax.broadcasted_iota(jnp.int32, (8, 128), 1)
    counts = jnp.zeros((8, 128), jnp.int32)
    for row in range(8):
        counts = jnp.where(sub == row, count_ref[chunk // 2, (chunk % 2) * 8 + row], counts)
    return slot < counts


def prepare(frac_ref, base_ref, wx_ref, wy_ref, wz_ref, charge_of):
    def chunk_step(chunk, carry):
        rows = pl.ds(pl.multiple_of(chunk * 8, 8), 8)
        weights = spline_weights(frac_ref[0, rows, :])
        offset = (base_ref[0, rows, :] & 3) + 4
        charge = charge_of(chunk, rows)
        for position in range(8):
            window = pick(offset - position, weights)
            wx_ref[position, rows, :] = window if charge is None else window * charge
        for degree, weight in enumerate(spline_weights(frac_ref[1, rows, :])):
            wy_ref[degree, rows, :] = weight
        for degree, weight in enumerate(spline_weights(frac_ref[2, rows, :])):
            wz_ref[degree, rows, :] = weight
        return carry

    lax.fori_loop(0, CELLS // 8, chunk_step, 0, unroll=4)


def cell_rows(ref, index, cell_x, cell_y):
    first = pl.multiple_of(cell_x * 16 + cell_y // 8 * 8, 8)
    return ref[index, pl.ds(first, 8), :][cell_y % 8 : cell_y % 8 + 1]


def depth_weights(base_ref, wz_ref, cell_x, cell_y):
    start = jnp.broadcast_to((cell_rows(base_ref, 2, cell_x, cell_y) - 2) & (NZ - 1), (8, 128))
    block, inside = start >> 5, start & 31
    weights = [
        jnp.broadcast_to(cell_rows(wz_ref, degree, cell_x, cell_y), (8, 128)) for degree in range(5)
    ]
    first = 4 + inside - lax.broadcasted_iota(jnp.int32, (8, 128), 0)
    highs, lows = [], []
    for step in range(5):
        window = pick(first - 8 * step, weights)
        high = window.astype(BF).astype(F32)
        highs.append(high)
        lows.append(window - high)
    parts = []
    zero = jnp.zeros((8, 128), F32)
    packed = []
    for value in (highs, lows):
        packed.append(
            [
                jnp.concatenate([value[0], value[1]], axis=0).astype(BF),
                jnp.concatenate([value[2], value[3]], axis=0).astype(BF),
                jnp.concatenate([value[4], zero], axis=0).astype(BF),
            ]
        )
    one = jnp.ones((8, 128), F32)
    hot = []
    for index in range(8):
        mark = jnp.where(block == index, one, 0.0)
        hot.append(jnp.concatenate([mark, mark], axis=0).astype(BF))
    for value in packed:
        pieces = []
        for index in range(8):
            pieces.append(value[0] * hot[index] + value[2] * hot[(index - 1) % 8])
            pieces.append(value[1] * hot[index])
        parts.append(jnp.concatenate(pieces, axis=0))
    return parts


def pair_depth(base_ref, wz_ref, cell_x, pair):
    first = depth_weights(base_ref, wz_ref, cell_x, 2 * pair)
    second = depth_weights(base_ref, wz_ref, cell_x, 2 * pair + 1)
    return (
        jnp.concatenate([first[0], second[0]], axis=1),
        jnp.concatenate([first[1], second[1]], axis=1),
    )


def pair_window_y(base_ref, wy_ref, cell_x, pair):
    parts = []
    for side in (0, 1):
        cell_y = 2 * pair + side
        position = lax.broadcasted_iota(jnp.int32, (16, 128), 0)
        selected = ((cell_rows(base_ref, 1, cell_x, cell_y) & 3) + 4 + 4 * side) - position
        weights = [cell_rows(wy_ref, degree, cell_x, cell_y) for degree in range(5)]
        parts.append(pick(selected, weights))
    return jnp.concatenate(parts, axis=1)


def pair_row(ref, position, cell_x, pair):
    return jnp.concatenate(
        [cell_rows(ref, position, cell_x, 2 * pair + side) for side in (0, 1)], axis=1
    )


def start_all(moves, sems):
    copies = [
        pltpu.make_async_copy(source, target, sems.at[index])
        for index, (source, target) in enumerate(moves)
    ]
    for copy in copies:
        copy.start()
    return copies


def spread_kernel(
    count_hbm,
    cot_hbm,
    frac_hbm,
    base_hbm,
    table_hbm,
    out_hbm,
    count_ref,
    cot_ref,
    frac_ref,
    base_ref,
    table_ref,
    out_ref,
    ext_ref,
    wx_ref,
    wy_ref,
    wz_ref,
    sems,
    out_sems,
):
    copies = start_all(
        [
            (count_hbm, count_ref),
            (cot_hbm, cot_ref),
            (frac_hbm, frac_ref),
            (base_hbm, base_ref),
            (table_hbm, table_ref),
        ],
        sems,
    )

    def clear(step, carry):
        rows = pl.ds(pl.multiple_of(step * EXT_Y, 8), EXT_Y)
        for half in (0, 1):
            ext_ref[half, rows, :] = jnp.zeros((EXT_Y, 128), F32)
        return carry

    lax.fori_loop(0, EXT_X, clear, 0, unroll=4)
    for copy in copies[:4]:
        copy.wait()

    def charge_of(chunk, rows):
        return jnp.where(occupied_rows(count_ref, chunk), cot_ref[rows, :], 0.0)

    prepare(frac_ref, base_ref, wx_ref, wy_ref, wz_ref, charge_of)

    def pair_work(cell_x, pair):
        depth_high, depth_low = pair_depth(base_ref, wz_ref, cell_x, pair)
        window_y = pair_window_y(base_ref, wy_ref, cell_x, pair)
        lifted = jnp.concatenate(
            [pair_row(wx_ref, u, cell_x, pair) * window_y for u in range(8)], axis=0
        )
        high, low = split(lifted)
        both = dot_nt(jnp.concatenate([high, low], axis=0), depth_high)
        patch = both[:128] + both[128:] + dot_nt(high, depth_low)
        for u in range(8):
            rows = pl.ds(pl.multiple_of((cell_x * 4 + u) * EXT_Y + pair * 8, 8), 16)
            for half in (0, 1):
                ext_ref[half, rows, :] += patch[16 * u : 16 * u + 16, 128 * half : 128 * half + 128]

    def cell_step(cell_x, carry):
        for pair in range(8):
            pair_work(cell_x, pair)
        return carry

    lax.fori_loop(0, 8, cell_step, 0)

    lane = lax.broadcasted_iota(jnp.int32, (128, 128), 1)

    def transform(blocks, first_row):
        high, low = split(jnp.concatenate(blocks, axis=0))
        both = dot_nt(table_ref[...], high)
        planes = both[:256] + both[256:] + dot_nt(table_ref[:256], low)
        for duo in (0, 1):
            first = planes[:128, 128 * duo : 128 * duo + 128]
            second = planes[128:, 128 * duo : 128 * duo + 128]
            left = jnp.where(lane < 64, first, pltpu.roll(second, 64, 1))
            right = jnp.where(lane < 64, pltpu.roll(first, 64, 1), second)
            out_ref[pl.ds(first_row + 2 * duo, 128, stride=ROWS), :] = left
            out_ref[pl.ds(first_row + 2 * duo + 1, 128, stride=ROWS), :] = right

    def send(index):
        rows = pl.ds(8 * index, 8)
        copy = pltpu.make_async_copy(
            out_ref.reshape(DEVICES, ROWS, 128).at[:, rows, :],
            out_hbm.at[:, rows, :],
            out_sems.at[index],
        )
        copy.start()
        return copy

    copies[4].wait()
    sends = []
    for step in range(9):
        blocks = []
        for row in range(4):
            rows = pl.ds((step * 4 + row) * EXT_Y, 64)
            blocks.append(jnp.concatenate([ext_ref[0, rows, :], ext_ref[1, rows, :]], axis=1))
        transform(blocks, step * 4)
        if step % 2 == 1:
            sends.append(send(step // 2))
    blocks = []
    for rim in range(4):
        rows = pl.ds(64 + rim, EXT_X, stride=EXT_Y)
        block = jnp.concatenate([ext_ref.at[0][rows, :], ext_ref.at[1][rows, :]], axis=1)
        blocks.append(jnp.concatenate([block, jnp.zeros((24, 256), F32)], axis=0))
    transform(blocks, 36)
    sends.append(send(4))
    for copy in sends:
        copy.wait()


def sort_kernel(
    flag_ref,
    influence_hbm,
    zero_hbm,
    sort_hbm,
    tables_hbm,
    weight_hbm,
    kept_hbm,
    sort,
    influence,
    zero_plane,
    weight_ref,
    tables,
    sems,
):
    plane, middle = flag_ref[0], flag_ref[1]
    moves = [(sort_hbm, sort)]
    for part in range(4):
        columns = pl.ds(128 * part, 128)
        moves.append((influence_hbm.at[plane, :, columns], influence.at[part]))
        moves.append((zero_hbm.at[:, columns], zero_plane.at[part, pl.ds(0, HALF_ROWS), :]))
    moves.append((tables_hbm, tables))
    copies = start_all(moves, sems)
    for copy in copies:
        copy.wait()

    def sorted_rows(planes, f, count):
        rows = pl.ds(f, 256, stride=2)
        value = jnp.concatenate([planes.at[part][rows, :] for part in range(4)], axis=1)
        if count < 256:
            value = jnp.where(lax.broadcasted_iota(jnp.int32, value.shape, 0) < count, value, 0.0)
        high, low = split(value)
        return dot(high, sort[...]) + dot(low, sort[...])

    @pl.when(middle == 0)
    def _plain():
        for f in (0, 1):
            own = sorted_rows(influence, f, 256)
            for residue in range(4):
                weight_ref[4 * f + residue] = own[:, 128 * residue : 128 * residue + 128]
        for which in range(8):
            weight_ref[8 + which] = jnp.zeros((256, 128), F32)

    @pl.when(middle != 0)
    def _mixed():
        index = lax.broadcasted_iota(jnp.int32, (256, 128), 0)
        for f in (0, 1):
            own = sorted_rows(influence, f, 256)
            half = sorted_rows(zero_plane, f, HALF_ROWS // 2)
            left = tables[pl.ds(TURN_START + 256 * f, 256), :]
            high, low = split(half)
            high, low = split(dot(left, high) + dot(left, low))
            for residue in range(4):
                which = 4 * f + residue
                columns = slice(128 * residue, 128 * residue + 128)
                other = (4 - residue) % 4
                partner = slice(128 * other, 128 * other + 128)
                right = tables[pl.ds(TURN_START + 512 + 256 * (residue > 0), 128), :][:, :128]
                turned = dot(high[:, partner], right) + dot(low[:, partner], right)
                whole = jnp.where(index <= 128 - f, half[:, columns], turned)
                weight_ref[which] = (own[:, columns] + whole) * 0.5
                weight_ref[8 + which] = (own[:, columns] - whole) * 0.5

    pltpu.sync_copy(weight_ref, weight_hbm.at[pl.ds(0, 16)])
    pltpu.sync_copy(tables, kept_hbm.at[pl.ds(0, TABLE_ROWS), :])


def plane_kernel(
    flag_ref,
    in_ref,
    weight_hbm,
    tables_hbm,
    out_ref,
    weight_ref,
    tables,
    block_high,
    block_low,
    rim_high,
    rim_low,
    spectrum,
    result,
    sems,
):
    middle = flag_ref[1]

    def table_move(first, count):
        rows = pl.ds(first, count)
        return tables_hbm.at[rows, :], tables.at[rows, :]

    moves = [
        table_move(0, Y_ROWS),
        table_move(X_START, 2048),
        (weight_hbm.at[pl.ds(0, 8)], weight_ref.at[pl.ds(0, 8)]),
        table_move(TURN_START, TURN_ROWS),
        (weight_hbm.at[pl.ds(8, 8)], weight_ref.at[pl.ds(8, 8)]),
        table_move(X_START + 2048, 1024),
    ]
    copies = [
        pltpu.make_async_copy(source, target, sems.at[index])
        for index, (source, target) in enumerate(moves)
    ]
    for copy in (*copies[:3], copies[5]):
        copy.start()

    @pl.when(middle != 0)
    def _more():
        for copy in copies[3:5]:
            copy.start()

    sub = lax.broadcasted_iota(jnp.int32, (8, 128), 0)
    turn_sign = jnp.where(lax.broadcasted_iota(jnp.int32, (32, 128), 1) < 64, -1.0, 1.0)

    def times_i(value):
        return pltpu.roll(value, 64, 1) * turn_sign[: value.shape[0]]

    def block_rows(p, q, first, count):
        return pl.ds((p * PY + q) * ROWS + first, count)

    def rim_rows(p):
        tiles = []
        for q in range(0, PY, 2):
            even = in_ref[block_rows(p, q, 32, 8), :]
            odd = in_ref[block_rows(p, q + 1, 32, 8), :]
            tiles.append(jnp.where(sub < 4, pltpu.roll(even, 4, 0), odd))
        tiles.append(jnp.zeros((96, 128), F32))
        return jnp.concatenate(tiles, axis=0).T

    def main_rows(p, q):
        own = in_ref[block_rows(p, q, 0, 32), :]
        edge = in_ref[block_rows((p + PX - 1) % PX, q, 32, 8), :]
        return jnp.concatenate([own[:8] + jnp.where(sub < 4, edge, 0.0), own[8:]], axis=0)

    turned_rims = {p: rim_rows(p) for p in (7, 15)}

    def edge_rows(p):
        before = turned_rims[(p + PX - 1) % PX]
        if p not in turned_rims:
            turned_rims[p] = rim_rows(p)
        turned = turned_rims[p]
        own = turned[0:32] + pltpu.roll(turned[64:96], 32, 1)
        edge = before[32:40] + pltpu.roll(before[96:104], 32, 1)
        first = own[:8] + jnp.where(sub < 4, edge, 0.0)
        return jnp.concatenate([first, own[8:]], axis=0)

    for p in range(8):
        rows = pl.ds(p * 32, 32)
        for q in range(2):
            columns = pl.ds(128 * q, 128)
            near = [main_rows(p, 2 * t + q) for t in range(4)]
            far = [main_rows(p + 8, 2 * t + q) for t in range(4)]
            for f, sign in ((0, 1.0), (1, -1.0)):
                a = [x + sign * y for x, y in zip(near, far)]
                sum_even, sum_odd = a[0] + a[2], a[1] + a[3]
                diff_even, diff_odd = a[0] - a[2], times_i(a[1] - a[3])
                parts = (
                    sum_even + sum_odd,
                    diff_even - diff_odd,
                    sum_even - sum_odd,
                    diff_even + diff_odd,
                )
                for residue, value in enumerate(parts):
                    high, low = split(value)
                    block_high[4 * f + residue, rows, columns] = high
                    block_low[4 * f + residue, rows, columns] = low
        near, far = edge_rows(p), edge_rows(p + 8)
        for f, value in ((0, near + far), (1, near - far)):
            rim_high[f, rows, :], rim_low[f, rows, :] = split(value)

    def y_table(residue, part):
        return tables[pl.ds((2 * residue + part) * 384, 384), :]

    def x_table(index):
        return pl.ds(X_START + 1024 * index, 1024)

    def left_products(rows, value):
        table = tables[rows, :]
        high, low = split(value)
        both = dot(table, high)
        total = both[:512] + both[512:] + dot(table[:512], low)
        return total[:256], total[256:]

    blocks = [(f, residue) for f in (0, 1) for residue in range(4)]
    copies[0].wait()
    for f, residue in blocks:
        which = 4 * f + residue
        high = jnp.concatenate([block_high[which], rim_high[f]], axis=1)
        low = jnp.concatenate([block_low[which], rim_low[f]], axis=1)
        both = dot(jnp.concatenate([high, low], axis=0), y_table(residue, 0))
        along_y = both[:256] + both[256:] + dot(high, y_table(residue, 1))
        if which == 0:
            copies[1].wait()
        cosine, sine = left_products(x_table(f), along_y)
        spectrum[which, :, :128] = cosine[:, :128] + sine[:, 128:]
        spectrum[which, :, 128:] = cosine[:, 128:] - sine[:, :128]

    copies[2].wait()
    copies[5].wait()

    @pl.when(middle == 0)
    def _scale():
        for which in range(8):
            for part in (0, 1):
                spectrum[which, :, pl.ds(128 * part, 128)] *= weight_ref[which]

    @pl.when(middle != 0)
    def _scale_mixed():
        copies[3].wait()
        copies[4].wait()
        for f in (0, 1):
            left = tables[pl.ds(TURN_START + 256 * f, 256), :]
            turned = []
            for residue in range(4):
                right = tables[pl.ds(TURN_START + 512 + 256 * (residue > 0), 256), :]
                high, low = split(spectrum[4 * f + (4 - residue) % 4])
                high, low = split(dot(left, high) + dot(left, low))
                turned.append(dot(high, right) + dot(low, right))
            for residue in range(4):
                which = 4 * f + residue
                for part, sign in ((0, 1.0), (1, -1.0)):
                    columns = pl.ds(128 * part, 128)
                    spectrum[which, :, columns] = (
                        spectrum[which, :, columns] * weight_ref[which]
                        + sign * turned[residue][:, 128 * part : 128 * part + 128] * weight_ref[8 + which]
                    )

    for f, residue in blocks:
        which = 4 * f + residue
        cosine, sine = left_products(x_table(2 * f), spectrum[which])
        back = jnp.concatenate(
            [cosine[:, :128] - sine[:, 128:], cosine[:, 128:] + sine[:, :128]], axis=1
        )
        high, low = split(back)
        both = dot_nt(jnp.concatenate([high, low], axis=0), y_table(residue, 0))
        result[which] = both[:256] + both[256:] + dot_nt(high, y_table(residue, 1))

    def chunk_copy(p):
        rows = pl.ds(p * PY * ROWS, PY * ROWS)
        return pltpu.make_async_copy(out_ref.at[rows, :], out_hbm.at[rows, :], out_sems.at[p])

    def quarters(first, count, columns):
        found = []
        for f in (0, 1):
            a = [result[4 * f + residue, pl.ds(first, count), columns] for residue in range(4)]
            sum_even, sum_odd = a[0] + a[2], a[1] + a[3]
            diff_even, diff_odd = a[0] - a[2], times_i(a[1] - a[3])
            found.append(
                (
                    sum_even + sum_odd,
                    diff_even + diff_odd,
                    sum_even - sum_odd,
                    diff_even - diff_odd,
                )
            )
        return found

    def total(first, count):
        rows, columns = pl.ds(first, count), pl.ds(256, 128)
        return [
            (result[4 * f, rows, columns] + result[4 * f + 1, rows, columns])
            + (result[4 * f + 2, rows, columns] + result[4 * f + 3, rows, columns])
            for f in (0, 1)
        ]

    for p in range(8):
        first, after = p * 32, ((p + 1) % 8) * 32
        wrap = -1.0 if p == 7 else 1.0
        own, edge = total(first, 32), total(after, 8)
        rims = []
        for sign in (1.0, -1.0):
            tall = jnp.concatenate(
                [own[0] + sign * own[1], edge[0] + (sign * wrap) * edge[1], jnp.zeros((88, 128), F32)],
                axis=0,
            ).T
            rims.append(tall[0:32] + pltpu.roll(tall[32:64], 64, 1))
        for q in range(2):
            columns = pl.ds(128 * q, 128)
            own, edge = quarters(first, 32, columns), quarters(after, 8, columns)
            for t in range(4):
                target_q = 2 * t + q
                for far, sign in ((0, 1.0), (8, -1.0)):
                    target_p = p + far
                    out_ref[block_rows(target_p, target_q, 0, 32), :] = own[0][t] + sign * own[1][t]
                    x_rim = edge[0][t] + (sign * wrap) * edge[1][t]
                    tile = rims[far // 8][8 * (target_q // 2) : 8 * (target_q // 2) + 8]
                    if target_q % 2 == 0:
                        tile = pltpu.roll(tile, 4, 0)
                    out_ref[block_rows(target_p, target_q, 32, 8), :] = jnp.where(
                        sub < 4, x_rim, tile
                    )


def atoms_kernel(
    first_step,
    frac_hbm,
    base_hbm,
    table_hbm,
    depth_ref,
    window_out,
    frac_ref,
    base_ref,
    table_ref,
    wx_ref,
    wy_ref,
    wz_ref,
    sems,
):
    step = pl.program_id(0) + first_step

    @pl.when(step == first_step)
    def _first():
        moves = [(frac_hbm, frac_ref), (base_hbm, base_ref), (table_hbm, table_ref)]
        for copy in start_all(moves, sems):
            copy.wait()
        prepare(frac_ref, base_ref, wx_ref, wy_ref, wz_ref, lambda chunk, rows: None)

    for index in range(8):
        high, low = pair_depth(base_ref, wz_ref, step, index)
        both = dot(table_ref[...], high)
        depth_ref[index, 0], depth_ref[index, 1] = split(
            both[:256] + both[256:] + dot(table_ref[:256], low)
        )
        window_out[index, pl.ds(8, 16), :] = pair_window_y(base_ref, wy_ref, step, index)
        for u in range(8):
            window_out[index, pl.ds(u, 1), :] = pair_row(wx_ref, u, step, index)


def gather_kernel(
    count_hbm,
    in_ref,
    *refs,
):
    depth_refs, window_refs = refs[:ATOM_PARTS], refs[ATOM_PARTS : 2 * ATOM_PARTS]
    out_ref, count_ref, late_ref, ext_ref, sems = refs[2 * ATOM_PARTS :]
    moves = [(count_hbm, count_ref)]
    for row in range(4):
        late = pl.ds(8 * row, 8)
        moves.append((depth_refs[-1].at[late], late_ref.at[late]))
    copies = start_all(moves, sems)
    depth_refs = (*depth_refs[:-1], late_ref)

    def turned(row):
        block = in_ref[pl.ds(row, 128, stride=ROWS), :].T
        return block[:64], block[64:]

    def row_step(row, carry):
        rows = pl.ds(pl.multiple_of(row * EXT_Y, 8), 64)
        last = pl.ds(pl.multiple_of(row * EXT_Y + 64, 8), 8)
        first, second = turned(row)
        ext_ref[0, rows, :] = first
        ext_ref[1, rows, :] = second
        for half in (0, 1):
            ext_ref[half, last, :] = jnp.zeros((8, 128), F32)
        return carry

    lax.fori_loop(0, 36, row_step, 0, unroll=6)
    for rim in range(4):
        rows = pl.ds(64 + rim, EXT_X, stride=EXT_Y)
        first, second = turned(36 + rim)
        ext_ref.at[0][rows, :] = first[:EXT_X]
        ext_ref.at[1][rows, :] = second[:EXT_X]
    copies[0].wait()

    def pair_work(cell_x, pair):
        index = cell_x * 8 + pair
        part = min(cell_x // 2, 2)
        depth_ref, window_ref = depth_refs[part], window_refs[part]
        inner = index - 16 * part
        windows = []
        for u in range(8):
            rows = pl.ds(pl.multiple_of((cell_x * 4 + u) * EXT_Y + pair * 8, 8), 16)
            windows.append(jnp.concatenate([ext_ref[0, rows, :], ext_ref[1, rows, :]], axis=1))
        high, low = split(jnp.concatenate(windows, axis=0))
        both = dot(jnp.concatenate([high, low], axis=0), depth_ref[inner, 0])
        patch = both[:128] + both[128:] + dot(high, depth_ref[inner, 1])
        total = patch[:16] * window_ref[inner, pl.ds(0, 1), :]
        for u in range(1, 8):
            total += patch[16 * u : 16 * u + 16] * window_ref[inner, pl.ds(u, 1), :]
        total = jnp.sum(total * window_ref[inner, pl.ds(8, 16), :], axis=0, keepdims=True)
        out_ref[pl.ds(index * 2, 1), :] = total[:, :128]
        out_ref[pl.ds(index * 2 + 1, 1), :] = total[:, 128:]

    for cell_x in range(8):
        if cell_x >= 4:
            copies[cell_x - 3].wait()
        for pair in range(8):
            pair_work(cell_x, pair)

    def mask_step(chunk, carry):
        rows = pl.ds(pl.multiple_of(chunk * 8, 8), 8)
        out_ref[rows, :] = jnp.where(occupied_rows(count_ref, chunk), out_ref[rows, :], 0.0)
        return carry

    lax.fori_loop(0, CELLS // 8, mask_step, 0, unroll=2)


VMEM = pl.BlockSpec(memory_space=pltpu.VMEM)
SMEM = pl.BlockSpec(memory_space=pltpu.SMEM)
HBM = pl.BlockSpec(memory_space=pltpu.HBM)
MIB = 1024 * 1024


def scratch(shape, dtype=F32):
    return pltpu.VMEM(shape, dtype)


def dmas(count):
    return pltpu.SemaphoreType.DMA((count,))


def params(mib):
    return pltpu.CompilerParams(vmem_limit_bytes=mib * MIB)


def cost(flops):
    return pl.CostEstimate(flops=flops, bytes_accessed=10**7, transcendentals=0)


ATOMS = (3, CELLS, 128)
WEIGHTS = [scratch((8, CELLS, 128)), scratch((5, CELLS, 128)), scratch((5, CELLS, 128))]
EXTENDED = scratch((2, EXT_X * EXT_Y, 128))


def per_device(cotangent, fraction, grid_base, cell_count, influence):
    device = lax.axis_index("px") * PY + lax.axis_index("py")
    flags = jnp.stack([(device < MIDDLE).astype(jnp.int32), (device == MIDDLE).astype(jnp.int32)])
    zero_plane = lax.ppermute(influence[0, :HALF_ROWS], ("px", "py"), [(0, MIDDLE)])
    fraction = fraction.reshape(ATOMS)
    grid_base = grid_base.reshape(ATOMS)
    forward_z, inverse_z = depth_tables()

    sent = pl.pallas_call(
        spread_kernel,
        out_shape=jax.ShapeDtypeStruct((DEVICES, ROWS, 128), F32),
        in_specs=[HBM] * 5,
        out_specs=HBM,
        scratch_shapes=[
            pltpu.SMEM((8, 16), jnp.int32),
            scratch((CELLS, 128)),
            scratch(ATOMS),
            scratch(ATOMS, jnp.int32),
            scratch((512, 256), BF),
            scratch((DEVICES * ROWS, 128)),
            EXTENDED,
            *WEIGHTS,
            dmas(5),
            dmas(5),
        ],
        compiler_params=params(62),
        cost_estimate=cost(10**10),
        name="spread",
    )(cell_count, cotangent.reshape(CELLS, 128), fraction, grid_base, forward_z)

    def exchange(array):
        return lax.all_to_all(array, ("px", "py"), split_axis=0, concat_axis=0, tiled=True)

    sent, zero_plane, fraction, grid_base = lax.optimization_barrier(
        (sent, zero_plane, fraction, grid_base)
    )
    planes = exchange(sent).reshape(DEVICES * ROWS, 128)
    weight, tables = pl.pallas_call(
        sort_kernel,
        out_shape=(
            jax.ShapeDtypeStruct((136, 256, 128), F32),
            jax.ShapeDtypeStruct((34816, 256), BF),
        ),
        in_specs=[SMEM] + [HBM] * 4,
        out_specs=(HBM, HBM),
        scratch_shapes=[
            scratch((512, 512), BF),
            scratch((4, 512, 128)),
            scratch((4, 512, 128)),
            scratch((16, 256, 128)),
            scratch((TABLE_ROWS, 256), BF),
            dmas(10),
        ],
        compiler_params=params(56),
        cost_estimate=cost(10**9),
        name="sort_influence",
    )(flags, influence, zero_plane, sort_table(), plane_tables())

    pairs = CELLS // 2
    depths, windows = [], []
    for first_step, steps, room in ATOM_CALLS:
        depth, window = pl.pallas_call(
            functools.partial(atoms_kernel, first_step),
            grid=(steps,),
            out_shape=(
                jax.ShapeDtypeStruct((room, 2, 256, 256), BF),
                jax.ShapeDtypeStruct((8 * steps, 24, 256), F32),
            ),
            in_specs=[HBM] * 3,
            out_specs=(
                pl.BlockSpec((8, 2, 256, 256), lambda i: (i, 0, 0, 0)),
                pl.BlockSpec((8, 24, 256), lambda i: (i, 0, 0)),
            ),
            scratch_shapes=[
                scratch(ATOMS),
                scratch(ATOMS, jnp.int32),
                scratch((512, 256), BF),
                *WEIGHTS,
                dmas(3),
            ],
            compiler_params=params(60),
            cost_estimate=cost(3 * 10**9),
            name="atoms",
        )(fraction, grid_base, inverse_z)
        depths.append(depth)
        windows.append(window)

    planes, depths, windows = lax.optimization_barrier((planes, depths, windows))
    back = pl.pallas_call(
        plane_kernel,
        out_shape=jax.ShapeDtypeStruct((DEVICES * ROWS, 128), F32),
        in_specs=[SMEM, VMEM, HBM, HBM],
        out_specs=VMEM,
        scratch_shapes=[
            scratch((16, 256, 128)),
            scratch((TABLE_ROWS, 256), BF),
            scratch((8, 256, 256), BF),
            scratch((8, 256, 256), BF),
            scratch((2, 256, 128), BF),
            scratch((2, 256, 128), BF),
            scratch((8, 256, 256)),
            scratch((8, 256, 384)),
            dmas(6),
        ],
        compiler_params=params(48),
        name="planes",
    )(flags, planes, weight, tables)
    returned = exchange(back.reshape(DEVICES, ROWS, 128)).reshape(DEVICES * ROWS, 128)

    gradient = pl.pallas_call(
        gather_kernel,
        out_shape=jax.ShapeDtypeStruct((CELLS, 128), F32),
        in_specs=[HBM] + [VMEM] * ATOM_PARTS + [HBM] + [VMEM] * ATOM_PARTS,
        out_specs=VMEM,
        scratch_shapes=[
            pltpu.SMEM((8, 16), jnp.int32),
            scratch((pairs // 2, 2, 256, 256), BF),
            EXTENDED,
            dmas(5),
        ],
        compiler_params=params(40),
        name="gather",
    )(cell_count, returned, *depths, *windows)
    return gradient.reshape(cotangent.shape)


def solution(mesh):
    placed = (
        P("px", "py", None),
        P(None, "px", "py", None),
        P(None, "px", "py", None),
        P("px", "py"),
        P(("px", "py"), None, None),
    )
    return jax.shard_map(
        per_device, mesh=mesh, in_specs=placed, out_specs=P("px", "py", None), check_vma=False
    )
```
